512 devices in a mesh: rows: 64 (over y, z), probes: 8 (over x, core).
Axes of the slice: x: 4, y: 4, z: 16, core: 2. Of those that a mesh axis runs over, the one named last changes fastest.
Arguments:
- probes: bfloat16 [128, 64, 256], P('rows', 'probes'), parts along dimension 1, may hold values from -6 to 6
- factor: bfloat16 [128, 4, 256, 256], P('rows'), may hold values from -0.125 to 0.125
- inverses: bfloat16 [128, 256, 256], P('rows')
- pattern: int32 [128, 4], replicated, may hold values from -1 to 95, as said below
- owner: int32 [128], replicated, may hold values from 0 to 127, each once
Outputs:
- solution: bfloat16 [128, 64, 256], P('rows', 'probes'), parts along dimension 1
- selected: bfloat16 [128, 40, 256, 256], P('rows', 'probes'), parts along dimension 1
The draws below stay inside these ranges and needn't reach their ends.
There are 8 independent parts, one for each index of `probes`. The reference program is written for one: setup_inputs(seed, part) draws one part's arguments, and reference() takes and returns one part's arrays. A program takes and returns all parts, laid end to end along the dimension named above; an argument that names none is the same for every part. Nothing has to cross between parts.
Inputs may be any that keep to these rules, and one draw needn't show every extreme that they name: `pattern`: Block-rows of the first level have only -1; every other block-row i names 4 different block-columns, all in levels below the level of i, one of them the block-row just before the first block-row of its own level.
All inputs are finite; a program needn't handle non-finite values.
Results may differ from the reference program's by a relative error of at most 0.012.
Values may be sent and summed in bfloat16 or wider, within the bound.
No kernel may reach another device: no remote copies, remote signals or barrier semaphores. Data moves between devices by JAX's collectives and lax.ppermute only.
A program may use at most 64 MiB of HBM per device.

```python
import math
import jax
import jax.numpy as jnp
from jax import lax

BLOCK = 256
PROBES = 8
ROWS_DEV = 2
NEIGHBORS = 4
LEVELS = 4
N_BLOCKROWS = 128


def draw_inverses(key, part):
    key = jax.random.fold_in(key, 23)
    first, second = jax.random.split(key)
    diag = jax.random.uniform(first, (N_BLOCKROWS, BLOCK), minval=0.6, maxval=1.0)
    off = jax.random.normal(second, (N_BLOCKROWS, BLOCK, BLOCK)) * (0.35 / math.sqrt(BLOCK))
    eye = jnp.eye(BLOCK, dtype=jnp.float32)
    return (off + eye[None] * diag[:, :, None]).astype(jnp.bfloat16)


def draw_pattern(key, part):
    key = jax.random.fold_in(key, 11)
    width = N_BLOCKROWS // LEVELS
    rows_all = jnp.arange(N_BLOCKROWS, dtype=jnp.int32)
    limits = rows_all // width * width
    keys = jax.random.split(key, N_BLOCKROWS)

    def one_row(row_key, limit):
        scores = jax.random.permutation(row_key, N_BLOCKROWS).astype(jnp.int32)
        masked = jnp.where(rows_all < limit, scores, scores + N_BLOCKROWS)
        masked = jnp.where(rows_all == limit - 1, -1, masked).astype(jnp.int32)
        picked = lax.top_k(-masked, NEIGHBORS)[1].astype(jnp.int32)
        return jnp.where(limit > 0, picked, -1).astype(jnp.int32)
    return jax.vmap(one_row)(keys, limits)


def steps_of(key, shape, cuts, least, top_value):
    def one(axis_at, parts):
        draws = jax.random.uniform(jax.random.fold_in(jax.random.fold_in(key, 6), axis_at), (parts,), jnp.float32, least / len(cuts), top_value / len(cuts))
        return jnp.repeat(jnp.exp(draws), shape[axis_at] // parts).reshape((-1,) + (1,) * (len(shape) - axis_at - 1))

    level = one(*cuts[0])
    for cut in cuts[1:]:
        level = level * one(*cut)
    return level


def scatter_about(stream_key, shape, spread, most, cuts=(), kind=jnp.bfloat16):
    values = jax.random.normal(stream_key, shape, jnp.float32) * spread
    if len(cuts) > 0:
        values = steps_of(stream_key, shape, cuts, -0.22, 0.18) * values
    return jnp.clip(values, min=-most, max=most).astype(kind)


def setup_inputs(seed: int = 0, part: int = 0) -> dict:
    arg_keys = jax.random.split(jax.random.key(seed), 6)
    own_keys = jax.random.split(jax.random.fold_in(arg_keys[5], part), 6)
    probes = scatter_about(own_keys[0], (N_BLOCKROWS, PROBES, BLOCK), 1.0, 6.0, ((0, 64),))
    factor = scatter_about(arg_keys[1], (N_BLOCKROWS, NEIGHBORS, BLOCK, BLOCK), (2 * BLOCK * NEIGHBORS) ** -0.5, 0.125, ((0, 64),))
    inverses = draw_inverses(jax.random.fold_in(arg_keys[5], 71), part)
    pattern = draw_pattern(jax.random.fold_in(arg_keys[5], 71), part)
    owner = jax.random.permutation(arg_keys[4], N_BLOCKROWS).astype(jnp.int32)
    return {"probes": probes, "factor": factor, "inverses": inverses, "pattern": pattern, "owner": owner}


def reference(probes, factor, inverses, pattern, owner):
    f32 = jnp.float32
    bf16 = jnp.bfloat16
    groups = N_BLOCKROWS // ROWS_DEV
    width = N_BLOCKROWS // LEVELS
    solved = jnp.zeros((N_BLOCKROWS, PROBES, BLOCK), bf16)
    for row in range(N_BLOCKROWS):
        slot = owner[row]
        cols = pattern[row]
        valid = cols >= 0
        safe = jnp.maximum(cols, 0).astype(jnp.int32)
        near = jnp.where(valid[:, None, None], solved[safe].astype(f32), jnp.zeros((), f32))
        partial_value = jnp.einsum("kpb,kab->pa", near, factor[slot].astype(f32))
        resid = (probes[slot].astype(f32) - partial_value).astype(bf16)
        value = jnp.dot(resid, inverses[slot].T, preferred_element_type=f32).astype(bf16)
        solved = solved.at[row].set(value)
    accum = jnp.zeros((N_BLOCKROWS, PROBES, BLOCK), f32)
    backed = jnp.zeros((N_BLOCKROWS, PROBES, BLOCK), bf16)
    for level in range(LEVELS - 1, -1, -1):
        rows_now = jnp.arange(level * width, (level + 1) * width, dtype=jnp.int32)
        slots = owner[rows_now]
        start = (solved[rows_now].astype(f32) - accum[rows_now]).astype(bf16)
        value = jnp.einsum("rpb,rba->rpa", start.astype(f32), inverses[slots].astype(f32)).astype(bf16)
        backed = backed.at[rows_now].set(value)
        if level > 0:
            cols = pattern[rows_now]
            valid = cols >= 0
            safe = jnp.maximum(cols, 0).astype(jnp.int32)
            terms = jnp.einsum("rpa,rkab->rkpb", value.astype(f32), factor[slots].astype(f32))
            terms = jnp.where(valid[:, :, None, None], terms, jnp.zeros((), f32))
            group = (slots // ROWS_DEV).astype(jnp.int32)
            group_all = jnp.broadcast_to(group[:, None], safe.shape)
            part = jnp.zeros((groups, N_BLOCKROWS, PROBES, BLOCK), f32).at[group_all, safe].add(terms)
            accum = accum + jnp.sum(part, axis=0)
    solution = jnp.zeros_like(backed).at[owner].set(backed)
    ordered = probes[owner]

    def one_row(row):
        cols = pattern[row]
        valid = cols >= 0
        safe = jnp.maximum(cols, 0).astype(jnp.int32)
        near = jnp.where(valid[:, None, None], ordered[safe].astype(f32), jnp.zeros((), f32))
        value = backed[row].astype(f32)
        off = jnp.einsum("pa,kpb->kab", value, near)
        diag = jnp.einsum("pa,pb->ab", value, ordered[row].astype(f32))
        return (jnp.concatenate([off, diag[None]], axis=0) / PROBES).astype(bf16)

    blocks = lax.map(one_row, jnp.arange(N_BLOCKROWS, dtype=jnp.int32))
    selected = jnp.zeros_like(blocks).at[owner].set(blocks)
    return solution, selected
```

```python
import jax
import jax.numpy as jnp
from jax import lax
from jax.sharding import Mesh, PartitionSpec as P

LEVELS = 4
Y, Z = 4, 16
ROWS = ("y", "z")


def body(probes, factor, inverses, pattern, owner):
    f32, bf16 = jnp.float32, jnp.bfloat16
    my, mz = lax.axis_index("y"), lax.axis_index("z")
    local, count, block = probes.shape
    total = owner.shape[0]
    width = total // LEVELS
    nbr = pattern.shape[1]
    pair = count // Y
    lanes = pair * block
    held = Y * local
    iota = jnp.arange(total, dtype=jnp.int32)

    def weights(d, l):
        return jnp.einsum("sab,skbc->skac", d, l, preferred_element_type=f32).astype(bf16)

    own_w = weights(inverses, factor)
    w = [own_w] + [
        lax.ppermute(own_w, "y", [(i, (i + d) % Y) for i in range(Y)]) for d in range(1, Y)
    ]
    q_own = jnp.einsum("spb,sab->spa", probes, inverses, preferred_element_type=f32).astype(bf16)

    def pick(keys, values):
        hit = keys[..., None] == iota
        return jnp.sum(jnp.where(hit, values, 0), axis=-1)

    def rows_of(slots):
        return jnp.sum(jnp.where(owner[None, :] == slots[:, None], iota[None, :], 0), axis=1)

    def sources(rows):
        hit = rows[:, None, None] == iota[None, :, None]
        cols = jnp.sum(jnp.where(hit, pattern[None], 0), axis=1)
        return jnp.where(cols >= 0, pick(cols, owner), -1)

    back = jnp.arange(Y, dtype=jnp.int32)
    local_iota = jnp.arange(local, dtype=jnp.int32)
    slots = (local * (((my - back) % Y) * Z + mz))[:, None] + local_iota[None, :]
    slots = slots.reshape(-1)
    rows = rows_of(slots)
    level = rows // width
    src = sources(rows).reshape(-1)
    sel = src[:, None] == iota[None, :]
    dev = src // local
    place = (dev % Z) * held + ((my - dev // Z) % Y) * local + src % local
    place = jnp.where(src >= 0, place, -1)
    sel_z = place[:, None] == iota[None, :]
    hold = slots[:, None] == iota[None, :]

    both = jnp.stack([q_own, probes]).reshape(2, local, Y, lanes)
    both = both.transpose(2, 0, 1, 3).reshape(Y, 1, 2 * local, lanes)
    both = jnp.broadcast_to(both, (Y, Z, 2 * local, lanes)).reshape(Y * Z, 2 * local, lanes)
    got = lax.all_to_all(both, ROWS, 0, 0, tiled=True)
    q_all = got[:, :local].reshape(total, lanes)
    p_all = got[:, local:].reshape(total, lanes)

    def choose(mask, table):
        return jnp.dot(mask.astype(bf16), table, preferred_element_type=f32)

    nat = (local * (back * Z + mz))[:, None] + local_iota[None, :]
    src_nat = sources(rows_of(nat.reshape(-1))).reshape(-1)
    near_p = choose(src_nat[:, None] == iota[None, :], p_all).astype(bf16)
    near_p = lax.all_to_all(near_p.reshape(Y, local * nbr, lanes), "y", 0, 0, tiled=True)
    near_p = near_p.reshape(Y, local, nbr, pair, block).transpose(1, 2, 0, 3, 4)
    near_p = near_p.reshape(local, nbr, count, block)

    q = choose(hold, q_all)
    solved = q.astype(bf16)
    known, mask = q_all, sel
    for lev in range(1, LEVELS):
        near = choose(mask, known).astype(bf16).reshape(Y, local, nbr, pair, block)
        moved = jnp.stack(
            [
                jnp.einsum("skcb,skab->sca", near[d], w[d], preferred_element_type=f32)
                for d in range(Y)
            ]
        ).reshape(held, lanes)
        value = (q - moved).astype(bf16)
        solved = jnp.where((level == lev)[:, None], value, solved)
        if lev < LEVELS - 1:
            send = jnp.broadcast_to(solved[None], (Z, held, lanes))
            known = lax.all_to_all(send, "z", 0, 0, tiled=True).reshape(total, lanes)
            mask = sel_z

    t = solved
    out = jnp.zeros((total, lanes), f32)
    for lev in range(LEVELS - 1, 0, -1):
        live = jnp.where((level == lev)[:, None], t, jnp.zeros((), bf16))
        live = live.reshape(Y, local, pair, block)
        terms = jnp.stack(
            [
                jnp.einsum("sca,skab->skcb", live[d], w[d], preferred_element_type=f32)
                for d in range(Y)
            ]
        ).reshape(held * nbr, lanes)
        m = sel_z if lev > 1 else sel
        if lev > 1:
            out = out + jnp.dot(m.T.astype(f32), terms, precision=lax.Precision.HIGHEST)
            got = lax.all_to_all(out.astype(bf16).reshape(Z, held, lanes), "z", 0, 0, tiled=True)
            acc = jnp.sum(got.astype(f32), axis=0)
            t = jnp.where((level == lev - 1)[:, None], (solved.astype(f32) - acc).astype(bf16), t)
        else:
            nat_out = out.reshape(Z, Y, local, lanes)
            nat_out = jnp.take(nat_out, (my - back) % Y, axis=1).transpose(1, 0, 2, 3)
            nat_out = nat_out.reshape(total, lanes)
            nat_out = nat_out + jnp.dot(m.T.astype(f32), terms, precision=lax.Precision.HIGHEST)
            level_all = rows_of(iota) // width
            nat_out = jnp.where((level_all == 0)[:, None], nat_out, 0.0)
            done = jnp.where((level > 0)[:, None], t, jnp.zeros((), bf16))
            nat_out = nat_out + jnp.dot(hold.T.astype(bf16), done, preferred_element_type=f32)
            got = lax.all_to_all(
                nat_out.astype(bf16).reshape(Y * Z, local, lanes), ROWS, 0, 0, tiled=True
            )
            got = jnp.sum(got.astype(f32).reshape(Y, Z, local, lanes), axis=1)
            got = got.reshape(Y, local, pair, block).transpose(1, 0, 2, 3)
            got = got.reshape(local, count, block)
    me = my * Z + mz
    my_level = rows_of(me * local + local_iota) // width
    first = (my_level == 0)[:, None, None]
    t_own = jnp.where(first, q_own.astype(f32) - got, got).astype(bf16)
    x = jnp.einsum("spa,sab->spb", t_own, inverses, preferred_element_type=f32).astype(bf16)
    near_all = jnp.concatenate([near_p, probes[:, None]], axis=1)
    selected = jnp.einsum("spa,skpb->skab", x, near_all, preferred_element_type=f32)
    return x, (selected / count).astype(bf16)


def solution(mesh):
    fine = Mesh(mesh.devices.reshape(Y, Z, -1), ("y", "z", "p"))
    return jax.shard_map(
        body,
        mesh=fine,
        in_specs=(
            P(ROWS, "p", None),
            P(ROWS, None, None, None),
            P(ROWS, None, None),
            P(),
            P(),
        ),
        out_specs=(P(ROWS, "p", None), P(ROWS, "p", None, None)),
        check_vma=False,
    )
```

```python
import functools

import jax
import jax.numpy as jnp
from jax import lax
from jax.experimental import pallas as pl
from jax.experimental.pallas import tpu as pltpu
from jax.sharding import Mesh, PartitionSpec as P

LEVELS = 4
Y, Z = 4, 16
LOCAL, COUNT, BLOCK, NBR = 2, 8, 256, 4
PAIR = COUNT // Y
HELD = Y * LOCAL
PAD = 8
WIDE = HELD * NBR * PAD
ROWS = ("y", "z")
F32, BF16 = jnp.float32, jnp.bfloat16
NT = (((1,), (1,)), ((), ()))
TN = (((0,), (0,)), ((), ()))
VMEM = pl.BlockSpec(memory_space=pltpu.VMEM)
SMEM = pl.BlockSpec(memory_space=pltpu.SMEM)


def call(kernel, out_shape, places, scratch=(), flops=0, moved=0):
    kinds = {"s": SMEM, "v": VMEM, "h": pl.BlockSpec(memory_space=pl.ANY)}
    return pl.pallas_call(
        kernel,
        out_shape=out_shape,
        in_specs=[kinds[p] for p in places],
        out_specs=jax.tree.map(lambda _: VMEM, out_shape),
        scratch_shapes=list(scratch),
        compiler_params=pltpu.CompilerParams(vmem_limit_bytes=52 * 2**20),
        cost_estimate=pl.CostEstimate(flops=flops, bytes_accessed=moved, transcendentals=0),
    )


def shape(*dims, dtype=BF16):
    return jax.ShapeDtypeStruct(dims, dtype)


def dot(a, b, dims=None):
    if dims is None:
        return jnp.dot(a, b, preferred_element_type=F32)
    return lax.dot_general(a, b, dims, preferred_element_type=F32)


def start_kernel(core_ref, probes_ref, inv_ref, factor_ref, q_ref, msg_ref, w_ref, d_ref, l_ref, sems):
    load_d = pltpu.make_async_copy(inv_ref, d_ref, sems.at[0])
    load_l = pltpu.make_async_copy(factor_ref.at[core_ref[0]], l_ref, sems.at[1])
    load_d.start()
    load_l.start()
    load_d.wait()
    parts = []
    for s in range(LOCAL):
        q = dot(probes_ref[s], d_ref[s], NT).astype(BF16)
        q_ref[s] = q
        parts.append(q.astype(F32))
    for s in range(LOCAL):
        parts.append(probes_ref[s].astype(F32))
    for y in range(Y):
        msg = jnp.concatenate([p[y * PAIR : (y + 1) * PAIR] for p in parts], axis=0).astype(BF16)
        for z in range(Z):
            msg_ref[y * Z + z] = msg
    load_l.wait()
    core = core_ref[0]
    d = d_ref[core]
    for k in range(NBR):
        w_ref[k] = dot(d, l_ref[k]).astype(BF16)


def load_rows(level_ref, lev, w_ref, held_ref, sems):
    waits = []
    for r in range(HELD):
        copy = pltpu.make_async_copy(w_ref.at[r], held_ref.at[r], sems.at[r])

        @pl.when(level_ref[r] == lev)
        def _():
            copy.start()

        waits.append(copy.wait)
    return waits


def forward_rows(level_ref, lev, waits, near_ref, q_ref, w_ref, solved_ref):
    for r in range(HELD):

        @pl.when(level_ref[r] == lev)
        def _():
            waits[r]()
            moved = jnp.zeros((PAD, BLOCK), F32)
            for k in range(NBR):
                at = (r * NBR + k) * PAD
                moved += dot(near_ref[at : at + PAD].astype(BF16), w_ref[r, k], NT)
            value = (q_ref[r * PAD : (r + 1) * PAD] - moved).astype(BF16).astype(F32)
            solved_ref[r * PAIR : (r + 1) * PAIR] = value[:PAIR]


def backward_rows(level_ref, lev, waits, t_ref, pad_ref, w_ref, terms_ref):
    terms_ref[...] = jnp.zeros_like(terms_ref)
    for r in range(HELD):

        @pl.when(level_ref[r] == lev)
        def _():
            if waits is not None:
                waits[r]()
            pad_ref[...] = jnp.zeros_like(pad_ref)
            pad_ref[:PAIR] = t_ref[r * PAIR : (r + 1) * PAIR]
            t = pad_ref[...].astype(BF16)
            for k in range(NBR):
                at = (r * NBR + k) * PAD
                terms_ref[at : at + PAD] = dot(t, w_ref[r, k])


def scatter(place, terms):
    high = terms.astype(BF16)
    low = (terms - high.astype(F32)).astype(BF16)
    return dot(place, high) + dot(place, low)


def broadcast_to_z(value, msg_ref):
    for z in range(Z):
        msg_ref[z] = value


def level1_kernel(level_ref, got_ref, pick_ref, w_ref, msg_ref, solved_ref, q_ref, near_p_ref, near_ref, held_ref, sems):
    waits = load_rows(level_ref, 1, w_ref, held_ref, sems)
    got = got_ref[...].reshape(Y * Z * 4 * PAIR, BLOCK)
    near_ref[...] = dot(pick_ref[:WIDE], got)
    q_ref[...] = dot(pick_ref[WIDE : WIDE + HELD * PAD], got)
    near_p = dot(pick_ref[WIDE + HELD * PAD :], got).astype(BF16)
    near_p_ref[...] = near_p.reshape(near_p_ref.shape)
    for r in range(HELD):
        solved_ref[r * PAIR : (r + 1) * PAIR] = q_ref[r * PAD : r * PAD + PAIR]
    forward_rows(level_ref, 1, waits, near_ref, q_ref, held_ref, solved_ref)
    broadcast_to_z(solved_ref[...].astype(BF16), msg_ref)


def level2_kernel(level_ref, got_ref, pick_ref, w_ref, q_ref, old_ref, msg_ref, solved_ref, near_ref, held_ref, sems):
    waits = load_rows(level_ref, 2, w_ref, held_ref, sems)
    near_ref[...] = dot(pick_ref[...], got_ref[...].reshape(Z * HELD * PAIR, BLOCK))
    solved_ref[...] = old_ref[...]
    forward_rows(level_ref, 2, waits, near_ref, q_ref, held_ref, solved_ref)
    broadcast_to_z(solved_ref[...].astype(BF16), msg_ref)


def level3_kernel(
    level_ref, got_ref, pick_ref, w_ref, q_ref, old_ref, put_ref,
    msg_ref, solved_ref, terms_ref, near_ref, pad_ref, held_ref, sems):
    waits = load_rows(level_ref, 3, w_ref, held_ref, sems)
    near_ref[...] = dot(pick_ref[...], got_ref[...].reshape(Z * HELD * PAIR, BLOCK))
    solved_ref[...] = old_ref[...]
    forward_rows(level_ref, 3, waits, near_ref, q_ref, held_ref, solved_ref)
    backward_rows(level_ref, 3, None, solved_ref, pad_ref, held_ref, terms_ref)
    out = scatter(put_ref[...], terms_ref[...])
    msg_ref[...] = out.astype(BF16).reshape(msg_ref.shape)


def finish_rows(level_ref, lev, got_ref, old_ref, t_ref):
    acc = jnp.sum(got_ref[...].astype(F32), axis=0)
    t_ref[...] = old_ref[...]
    for r in range(HELD):

        @pl.when(level_ref[r] == lev)
        def _():
            rows = slice(r * PAIR, (r + 1) * PAIR)
            t_ref[rows] = (old_ref[rows] - acc[rows]).astype(BF16).astype(F32)


def back2_kernel(
    level_ref, got_ref, w_ref, old_ref, before_ref, put_ref,
    msg_ref, t_ref, sums_ref, terms_ref, pad_ref, held_ref, sems):
    waits = load_rows(level_ref, 2, w_ref, held_ref, sems)
    finish_rows(level_ref, 2, got_ref, old_ref, t_ref)
    backward_rows(level_ref, 2, waits, t_ref, pad_ref, held_ref, terms_ref)
    sums_ref[...] = before_ref[...] + terms_ref[...]
    out = scatter(put_ref[...], sums_ref[...])
    msg_ref[...] = out.astype(BF16).reshape(msg_ref.shape)


def back1_kernel(
    level_ref, got_ref, w_ref, old_ref, before_ref, put_ref, own_ref, msg_ref, t_ref, terms_ref, pad_ref, held_ref, sems):
    waits = load_rows(level_ref, 1, w_ref, held_ref, sems)
    finish_rows(level_ref, 1, got_ref, old_ref, t_ref)
    backward_rows(level_ref, 1, waits, t_ref, pad_ref, held_ref, terms_ref)
    sums = before_ref[...] + terms_ref[...]
    t = t_ref[...].astype(BF16)
    half = BLOCK // 2
    left = scatter(put_ref[0], sums[:, :half]) + dot(own_ref[0], t[:, :half])
    right = scatter(put_ref[1], sums[:, half:]) + dot(own_ref[1], t[:, half:])
    msg_ref[...] = (left + right).astype(BF16).reshape(msg_ref.shape)


def final_kernel(first_ref, got_ref, q_ref, probes_ref, inv_ref, near_ref, x_ref, sel_ref):
    group = LOCAL * PAIR
    sums = []
    for y in range(Y):
        v = jnp.sum(got_ref[y * Z : (y + 1) * Z].astype(F32), axis=0)
        sums.append(jnp.concatenate([v[:group], v[group:]], axis=1))
    for s in range(LOCAL):
        acc = jnp.concatenate([v[s * PAIR : (s + 1) * PAIR] for v in sums], axis=0)
        base = jnp.where(first_ref[s] == 1, q_ref[s].astype(F32) - acc, acc)
        x = dot(base.astype(BF16), inv_ref[s]).astype(BF16)
        x_ref[s] = x
        for k in range(NBR):
            at = (s * NBR + k) * PAIR
            near = jnp.concatenate(
                [near_ref[y, at : at + PAIR].astype(F32) for y in range(Y)], axis=0
            ).astype(BF16)
            sel_ref[s, k] = (dot(x, near, TN) * (1.0 / COUNT)).astype(BF16)
        sel_ref[s, NBR] = (dot(x, probes_ref[s], TN) * (1.0 / COUNT)).astype(BF16)


def body(probes, factor, inverses, pattern, owner):
    my, mz = lax.axis_index("y"), lax.axis_index("z")
    total = owner.shape[0]
    width = total // LEVELS
    iota = jnp.arange(total, dtype=jnp.int32)

    core = lax.axis_index("c").reshape(1)
    w_shape = shape(NBR, BLOCK, BLOCK)
    out = (shape(LOCAL, COUNT, BLOCK), shape(Y * Z, 4 * PAIR, BLOCK), w_shape)
    scratch = [
        pltpu.VMEM((LOCAL, BLOCK, BLOCK), BF16),
        pltpu.VMEM((NBR, BLOCK, BLOCK), BF16),
        pltpu.SemaphoreType.DMA((2,)),
    ]
    q_own, msg, w_send = call(start_kernel, out, "svhh", scratch)(
        core, probes, inverses, factor
    )
    got = lax.all_to_all(msg, ROWS, 0, 0, tiled=True)
    w = lax.all_gather(w_send, ("y", "c"), axis=0, tiled=False)

    def rows_of(slots):
        return jnp.sum(jnp.where(owner[None, :] == slots[:, None], iota[None, :], 0), axis=1)

    local_iota = jnp.arange(LOCAL, dtype=jnp.int32)
    held_y = jnp.arange(Y, dtype=jnp.int32)
    slots = (LOCAL * (held_y * Z + mz))[:, None] + local_iota[None, :]
    slots = slots.reshape(-1)
    rows = rows_of(slots)
    level = rows // width
    hit = rows[:, None, None] == iota[None, :, None]
    cols = jnp.sum(jnp.where(hit, pattern[None], 0), axis=1)
    src = jnp.sum(jnp.where(cols[..., None] == iota, owner, 0), axis=-1)
    src = jnp.where(cols >= 0, src, -1).reshape(-1)
    dev = src // LOCAL
    bad = -(2**20)
    place_z = jnp.where(src >= 0, (dev % Z) * HELD + (dev // Z) * LOCAL + src % LOCAL, bad)

    def rows_at(place, pad, stride=PAIR):
        col = jnp.arange(pad, dtype=jnp.int32)
        at = jnp.where(col[None, :] < PAIR, place[:, None] * stride + col[None, :], bad)
        return at.reshape(-1)

    def hot(at, size):
        return (at[:, None] == jnp.arange(size, dtype=jnp.int32)[None, :]).astype(BF16)

    def first_at(slot, kind):
        return jnp.where(slot >= 0, (slot // LOCAL) * 4 + kind * LOCAL + slot % LOCAL, bad)

    pick1 = jnp.concatenate(
        [
            rows_at(first_at(src, 0), PAD),
            rows_at(first_at(slots, 0), PAD),
            rows_at(first_at(src, 1), PAIR),
        ]
    )
    pick1 = hot(pick1, Y * Z * 4 * PAIR)
    at_z = rows_at(place_z, PAD)
    pick_z = hot(at_z, Z * HELD * PAIR)
    put_z = (jnp.arange(Z * HELD * PAIR, dtype=jnp.int32)[:, None] == at_z[None, :]).astype(BF16)
    level_of_src = jnp.where(cols >= 0, cols // width, LEVELS).reshape(-1)
    group = LOCAL * PAIR

    def last_at(slot, good):
        return jnp.where(good, (slot // LOCAL) * (2 * LOCAL) + slot % LOCAL, bad)

    size = Y * Z * 2 * group
    last_rows = jnp.arange(size, dtype=jnp.int32)
    put_at = rows_at(last_at(src, level_of_src == 0), PAD)
    own_at = rows_at(last_at(slots, level > 0), PAIR)
    put_last = jnp.stack(
        [(last_rows[:, None] == (put_at + h * group)[None, :]) for h in range(2)]
    ).astype(BF16)
    own_last = jnp.stack(
        [(last_rows[:, None] == (own_at + h * group)[None, :]) for h in range(2)]
    ).astype(BF16)

    near_scratch = pltpu.VMEM((WIDE, BLOCK), F32)
    held_scratch = [
        pltpu.VMEM((HELD, NBR, BLOCK, BLOCK), BF16),
        pltpu.SemaphoreType.DMA((HELD,)),
    ]
    pad_scratch = pltpu.VMEM((PAD, BLOCK), F32)
    msg_z = shape(Z, HELD * PAIR, BLOCK)
    held = shape(HELD * PAIR, BLOCK, dtype=F32)
    sums = shape(WIDE, BLOCK, dtype=F32)
    out = (msg_z, held, shape(HELD * PAD, BLOCK, dtype=F32), shape(Y, LOCAL * NBR * PAIR, BLOCK))
    msg, solved, q, near_p = call(
        level1_kernel, out, "svv" + "h", [near_scratch] + held_scratch
    )(level, got, pick1, w)
    got = lax.all_to_all(msg, "z", 0, 0, tiled=True)
    near_p = lax.all_to_all(near_p, "y", 0, 0, tiled=True)
    msg, solved = call(
        level2_kernel, (msg_z, held), "svv" + "h" + "vv", [near_scratch] + held_scratch
    )(level, got, pick_z, w, q, solved)
    got = lax.all_to_all(msg, "z", 0, 0, tiled=True)
    msg, solved, before = call(
        level3_kernel,
        (msg_z, held, sums),
        "svv" + "h" + "vvv",
        [near_scratch, pad_scratch] + held_scratch,
    )(level, got, pick_z, w, q, solved, put_z)
    got = lax.all_to_all(msg, "z", 0, 0, tiled=True)
    msg, t, before = call(
        back2_kernel,
        (msg_z, held, sums),
        "sv" + "h" + "vvv",
        [near_scratch, pad_scratch] + held_scratch,
    )(level, got, w, solved, before, put_z)
    got = lax.all_to_all(msg, "z", 0, 0, tiled=True)
    msg, t = call(
        back1_kernel,
        (shape(Y * Z, 2 * group, BLOCK // 2), held),
        "sv" + "h" + "vvvv",
        [near_scratch, pad_scratch] + held_scratch,
    )(level, got, w, t, before, put_last, own_last)
    got = lax.all_to_all(msg, ROWS, 0, 0, tiled=True)
    mine = (my * Z + mz) * LOCAL + local_iota
    first = (rows_of(mine) < width).astype(jnp.int32)
    out = (shape(LOCAL, COUNT, BLOCK), shape(LOCAL, NBR + 1, BLOCK, BLOCK))
    return call(final_kernel, out, "svvvvv")(first, got, q_own, probes, inverses, near_p)


def solution(mesh):
    fine = Mesh(mesh.devices.reshape(Y, Z, -1, 2), ("y", "z", "x", "c"))
    parts = ("x", "c")
    return jax.shard_map(
        body,
        mesh=fine,
        in_specs=(
            P(ROWS, parts, None),
            P(ROWS, None, None, None),
            P(ROWS, None, None),
            P(),
            P(),
        ),
        out_specs=(P(ROWS, parts, None), P(ROWS, parts, None, None)),
        check_vma=False,
    )
```

```python
import functools

import jax
import jax.numpy as jnp
from jax import lax
from jax.experimental import pallas as pl
from jax.experimental.pallas import tpu as pltpu
from jax.sharding import Mesh, PartitionSpec as P

LEVELS = 4
Y, Z = 4, 16
LOCAL, COUNT, BLOCK, NBR = 2, 8, 256, 4
PAIR = COUNT // Y
HELD = Y * LOCAL
PAD = 8
WIDE = HELD * NBR * PAD
ROWS = ("y", "z")
F32, BF16 = jnp.float32, jnp.bfloat16
NT = (((1,), (1,)), ((), ()))
TN = (((0,), (0,)), ((), ()))
VMEM = pl.BlockSpec(memory_space=pltpu.VMEM)
SMEM = pl.BlockSpec(memory_space=pltpu.SMEM)


def call(kernel, out_shape, places, scratch=(), room=52):
    kinds = {"s": SMEM, "v": VMEM, "h": pl.BlockSpec(memory_space=pl.ANY)}
    return pl.pallas_call(
        kernel,
        out_shape=out_shape,
        in_specs=[kinds[p] for p in places],
        out_specs=jax.tree.map(lambda _: VMEM, out_shape),
        scratch_shapes=list(scratch),
        compiler_params=pltpu.CompilerParams(vmem_limit_bytes=room * 2**20),
    )


def shape(*dims, dtype=BF16):
    return jax.ShapeDtypeStruct(dims, dtype)


def dot(a, b, dims=None):
    if dims is None:
        return jnp.dot(a, b, preferred_element_type=F32)
    return lax.dot_general(a, b, dims, preferred_element_type=F32)


def start_kernel(core_ref, probes_ref, inv_ref, factor_ref, q_ref, msg_ref, w_ref, send_ref, p_ref, d_ref, l_ref, sems):
    load_p = pltpu.make_async_copy(probes_ref, p_ref, sems.at[2])
    load_d = pltpu.make_async_copy(inv_ref, d_ref, sems.at[0])
    load_l = pltpu.make_async_copy(factor_ref, l_ref, sems.at[1])
    load_p.start()
    load_d.start()
    load_l.start()
    load_p.wait()
    load_d.wait()
    parts = []
    for s in range(LOCAL):
        q = dot(p_ref[s], d_ref[s], NT).astype(BF16)
        q_ref[s] = q
        parts.append(q.astype(F32))
    for s in range(LOCAL):
        parts.append(p_ref[s].astype(F32))
    for y in range(Y):
        msg = jnp.concatenate([p[y * PAIR : (y + 1) * PAIR] for p in parts], axis=0).astype(BF16)
        for z in range(Z):
            msg_ref[y * Z + z] = msg
    load_l.wait()
    for i in range(LOCAL):
        slot = (core_ref[0] + i) % LOCAL
        for k in range(NBR):
            w = dot(d_ref[slot], l_ref[slot, k]).astype(BF16)
            w_ref[i, k] = w
            if i == 0:
                send_ref[k] = w


def load_rows(level_ref, lev, w_refs, held_ref, sems):
    waits = []
    for r in range(HELD):
        d, slot = r // LOCAL, r % LOCAL
        if d == 0:
            source = w_refs[0].at[slot]
        else:
            source = w_refs[slot * (Y - 1) + d]
        copy = pltpu.make_async_copy(source, held_ref.at[r], sems.at[r])

        @pl.when(level_ref[r] == lev)
        def _():
            copy.start()

        waits.append(copy.wait)
    return waits


def forward_rows(level_ref, lev, waits, near_ref, q_ref, w_ref, solved_ref):
    for r in range(HELD):

        @pl.when(level_ref[r] == lev)
        def _():
            waits[r]()
            moved = jnp.zeros((PAD, BLOCK), F32)
            for k in range(NBR):
                at = (r * NBR + k) * PAD
                moved += dot(near_ref[at : at + PAD].astype(BF16), w_ref[r, k], NT)
            value = (q_ref[r * PAD : (r + 1) * PAD] - moved).astype(BF16).astype(F32)
            solved_ref[r * PAIR : (r + 1) * PAIR] = value[:PAIR]


def backward_rows(level_ref, lev, waits, t_ref, pad_ref, w_ref, terms_ref):
    terms_ref[...] = jnp.zeros_like(terms_ref)
    for r in range(HELD):

        @pl.when(level_ref[r] == lev)
        def _():
            if waits is not None:
                waits[r]()
            pad_ref[...] = jnp.zeros_like(pad_ref)
            pad_ref[:PAIR] = t_ref[r * PAIR : (r + 1) * PAIR]
            t = pad_ref[...].astype(BF16)
            for k in range(NBR):
                at = (r * NBR + k) * PAD
                terms_ref[at : at + PAD] = dot(t, w_ref[r, k])


def scatter(place, terms):
    high = terms.astype(BF16)
    low = (terms - high.astype(F32)).astype(BF16)
    return dot(place, high) + dot(place, low)


def broadcast_to_z(value, msg_ref):
    for z in range(Z):
        msg_ref[z] = value


def neighbour_kernel(got_ref, pick_ref, near_ref):
    got = got_ref[...].reshape(Y * Z * 4 * PAIR, BLOCK)
    near_ref[...] = dot(pick_ref[...], got).astype(BF16).reshape(near_ref.shape)


def level1_kernel(level_ref, got_ref, pick_ref, w0_ref, w1_ref, w2_ref, w3_ref, w4_ref, w5_ref, w6_ref, msg_ref, solved_ref, q_ref, near_ref, held_ref, sems):
    waits = load_rows(level_ref, 1, (w0_ref, w1_ref, w2_ref, w3_ref, w4_ref, w5_ref, w6_ref), held_ref, sems)
    got = got_ref[...].reshape(Y * Z * 4 * PAIR, BLOCK)
    near_ref[...] = dot(pick_ref[:WIDE], got)
    q_ref[...] = dot(pick_ref[WIDE : WIDE + HELD * PAD], got)
    for r in range(HELD):
        solved_ref[r * PAIR : (r + 1) * PAIR] = q_ref[r * PAD : r * PAD + PAIR]
    forward_rows(level_ref, 1, waits, near_ref, q_ref, held_ref, solved_ref)
    broadcast_to_z(solved_ref[...].astype(BF16), msg_ref)


def level2_kernel(level_ref, got_ref, pick_ref, w0_ref, w1_ref, w2_ref, w3_ref, w4_ref, w5_ref, w6_ref, q_ref, old_ref, msg_ref, solved_ref, near_ref, held_ref, sems):
    waits = load_rows(level_ref, 2, (w0_ref, w1_ref, w2_ref, w3_ref, w4_ref, w5_ref, w6_ref), held_ref, sems)
    near_ref[...] = dot(pick_ref[...], got_ref[...].reshape(Z * HELD * PAIR, BLOCK))
    solved_ref[...] = old_ref[...]
    forward_rows(level_ref, 2, waits, near_ref, q_ref, held_ref, solved_ref)
    broadcast_to_z(solved_ref[...].astype(BF16), msg_ref)


def level3_kernel(
    level_ref, got_ref, pick_ref, w0_ref, w1_ref, w2_ref, w3_ref, w4_ref, w5_ref, w6_ref, q_ref, old_ref, put_ref,
    msg_ref, solved_ref, terms_ref, near_ref, pad_ref, held_ref, sems):
    waits = load_rows(level_ref, 3, (w0_ref, w1_ref, w2_ref, w3_ref, w4_ref, w5_ref, w6_ref), held_ref, sems)
    near_ref[...] = dot(pick_ref[...], got_ref[...].reshape(Z * HELD * PAIR, BLOCK))
    solved_ref[...] = old_ref[...]
    forward_rows(level_ref, 3, waits, near_ref, q_ref, held_ref, solved_ref)
    backward_rows(level_ref, 3, None, solved_ref, pad_ref, held_ref, terms_ref)
    out = scatter(put_ref[...], terms_ref[...])
    msg_ref[...] = out.astype(BF16).reshape(msg_ref.shape)


def finish_rows(level_ref, lev, got_ref, old_ref, t_ref):
    acc = jnp.sum(got_ref[...].astype(F32), axis=0)
    t_ref[...] = old_ref[...]
    for r in range(HELD):

        @pl.when(level_ref[r] == lev)
        def _():
            rows = slice(r * PAIR, (r + 1) * PAIR)
            t_ref[rows] = (old_ref[rows] - acc[rows]).astype(BF16).astype(F32)


def back2_kernel(
    level_ref, got_ref, w0_ref, w1_ref, w2_ref, w3_ref, w4_ref, w5_ref, w6_ref, old_ref, before_ref, put_ref,
    msg_ref, t_ref, sums_ref, terms_ref, pad_ref, held_ref, sems):
    waits = load_rows(level_ref, 2, (w0_ref, w1_ref, w2_ref, w3_ref, w4_ref, w5_ref, w6_ref), held_ref, sems)
    finish_rows(level_ref, 2, got_ref, old_ref, t_ref)
    backward_rows(level_ref, 2, waits, t_ref, pad_ref, held_ref, terms_ref)
    sums_ref[...] = before_ref[...] + terms_ref[...]
    out = scatter(put_ref[...], sums_ref[...])
    msg_ref[...] = out.astype(BF16).reshape(msg_ref.shape)


def back1_kernel(
    level_ref, got_ref, w0_ref, w1_ref, w2_ref, w3_ref, w4_ref, w5_ref, w6_ref, old_ref, before_ref, put_ref, own_ref, msg_ref, t_ref, terms_ref, pad_ref, held_ref, sems):
    waits = load_rows(level_ref, 1, (w0_ref, w1_ref, w2_ref, w3_ref, w4_ref, w5_ref, w6_ref), held_ref, sems)
    finish_rows(level_ref, 1, got_ref, old_ref, t_ref)
    backward_rows(level_ref, 1, waits, t_ref, pad_ref, held_ref, terms_ref)
    sums = before_ref[...] + terms_ref[...]
    t = t_ref[...].astype(BF16)
    half = BLOCK // 2
    left = scatter(put_ref[0], sums[:, :half]) + dot(own_ref[0], t[:, :half])
    right = scatter(put_ref[1], sums[:, half:]) + dot(own_ref[1], t[:, half:])
    msg_ref[...] = (left + right).astype(BF16).reshape(msg_ref.shape)


def final_kernel(first_ref, got_ref, q_ref, probes_ref, inv_ref, turn_ref, near0_ref, near1_ref, near2_ref, near3_ref, x_ref, sel_ref):
    near_refs = (near0_ref, near1_ref, near2_ref, near3_ref)
    group = LOCAL * PAIR
    sums = []
    for y in range(Y):
        v = jnp.sum(got_ref[y * Z : (y + 1) * Z].astype(F32), axis=0)
        sums.append(jnp.concatenate([v[:group], v[group:]], axis=1))
    for s in range(LOCAL):
        acc = jnp.concatenate([v[s * PAIR : (s + 1) * PAIR] for v in sums], axis=0)
        base = jnp.where(first_ref[s] == 1, q_ref[s].astype(F32) - acc, acc)
        x = dot(base.astype(BF16), inv_ref[s]).astype(BF16)
        x_ref[s] = x
        turned = dot(turn_ref[...], x).astype(BF16)
        for k in range(NBR):
            at = (s * NBR + k) * PAIR
            near = jnp.concatenate(
                [ref[at : at + PAIR].astype(F32) for ref in near_refs], axis=0
            ).astype(BF16)
            sel_ref[s, k] = (dot(turned, near, TN) * (1.0 / COUNT)).astype(BF16)
        sel_ref[s, NBR] = (dot(x, probes_ref[s], TN) * (1.0 / COUNT)).astype(BF16)


def body(probes, factor, inverses, pattern, owner):
    my, mz = lax.axis_index("y"), lax.axis_index("z")
    total = owner.shape[0]
    width = total // LEVELS
    iota = jnp.arange(total, dtype=jnp.int32)

    core = lax.axis_index("c").reshape(1)
    w_shape = shape(NBR, BLOCK, BLOCK)
    w_pair = shape(LOCAL, NBR, BLOCK, BLOCK)
    out = (shape(LOCAL, COUNT, BLOCK), shape(Y * Z, 4 * PAIR, BLOCK), w_pair, w_shape)
    scratch = [
        pltpu.VMEM((LOCAL, COUNT, BLOCK), BF16),
        pltpu.VMEM((LOCAL, BLOCK, BLOCK), BF16),
        pltpu.VMEM((LOCAL, NBR, BLOCK, BLOCK), BF16),
        pltpu.SemaphoreType.DMA((3,)),
    ]
    q_own, msg, w_own, w_send = call(start_kernel, out, "shhh", scratch, room=60)(
        core, probes, inverses, factor
    )
    def along(step):
        return lax.ppermute(w_send, "y", [(i, (i + step) % Y) for i in range(Y)])

    w_mine = [along(step) for step in (1, 2, 3)]
    got = lax.all_to_all(msg, ROWS, 0, 0, tiled=True)
    w_other = [lax.ppermute(v, "c", [(0, 1), (1, 0)]) for v in w_mine]
    ws = [w_own, *w_mine, *w_other]

    def rows_of(slots):
        return jnp.sum(jnp.where(owner[None, :] == slots[:, None], iota[None, :], 0), axis=1)

    local_iota = jnp.arange(LOCAL, dtype=jnp.int32)
    held_y = (my - jnp.arange(Y, dtype=jnp.int32)) % Y
    core = lax.axis_index("c")
    slots = (LOCAL * (held_y * Z + mz))[:, None] + (core + local_iota[None, :]) % LOCAL
    slots = slots.reshape(-1)
    rows = rows_of(slots)
    level = rows // width
    hit = rows[:, None, None] == iota[None, :, None]
    cols = jnp.sum(jnp.where(hit, pattern[None], 0), axis=1)
    src = jnp.sum(jnp.where(cols[..., None] == iota, owner, 0), axis=-1)
    src = jnp.where(cols >= 0, src, -1).reshape(-1)
    dev = src // LOCAL
    bad = -(2**20)
    turn = (my - dev // Z) % Y
    place_z = jnp.where(src >= 0, (dev % Z) * HELD + turn * LOCAL + (src - core) % LOCAL, bad)

    def rows_at(place, pad, stride=PAIR):
        col = jnp.arange(pad, dtype=jnp.int32)
        at = jnp.where(col[None, :] < PAIR, place[:, None] * stride + col[None, :], bad)
        return at.reshape(-1)

    def hot(at, size):
        return (at[:, None] == jnp.arange(size, dtype=jnp.int32)[None, :]).astype(BF16)

    def first_at(slot, kind):
        return jnp.where(slot >= 0, (slot // LOCAL) * 4 + kind * LOCAL + slot % LOCAL, bad)

    natural = (held_y[:, None] * Z + mz) * LOCAL + local_iota[None, :]
    nat_rows = rows_of(natural.reshape(-1))
    nat_cols = jnp.sum(jnp.where(nat_rows[:, None, None] == iota[None, :, None], pattern[None], 0), axis=1)
    nat_src = jnp.sum(jnp.where(nat_cols[..., None] == iota, owner, 0), axis=-1)
    nat_src = jnp.where(nat_cols >= 0, nat_src, -1).reshape(-1)
    pick1 = jnp.concatenate(
        [
            rows_at(first_at(src, 0), PAD),
            rows_at(first_at(slots, 0), PAD),
        ]
    )
    pick1 = hot(pick1, Y * Z * 4 * PAIR)
    pick_p = hot(rows_at(first_at(nat_src, 1), PAIR), Y * Z * 4 * PAIR)
    near_p = call(neighbour_kernel, shape(Y, LOCAL * NBR * PAIR, BLOCK), "vv")(got, pick_p)
    near_p = [near_p[0]] + [
        lax.ppermute(near_p[d], "y", [(i, (i - d) % Y) for i in range(Y)]) for d in range(1, Y)
    ]
    at_z = rows_at(place_z, PAD)
    pick_z = hot(at_z, Z * HELD * PAIR)
    put_z = (jnp.arange(Z * HELD * PAIR, dtype=jnp.int32)[:, None] == at_z[None, :]).astype(BF16)
    level_of_src = jnp.where(cols >= 0, cols // width, LEVELS).reshape(-1)
    group = LOCAL * PAIR

    def last_at(slot, good):
        return jnp.where(good, (slot // LOCAL) * (2 * LOCAL) + slot % LOCAL, bad)

    size = Y * Z * 2 * group
    last_rows = jnp.arange(size, dtype=jnp.int32)
    put_at = rows_at(last_at(src, level_of_src == 0), PAD)
    own_at = rows_at(last_at(slots, level > 0), PAIR)
    put_last = jnp.stack(
        [(last_rows[:, None] == (put_at + h * group)[None, :]) for h in range(2)]
    ).astype(BF16)
    own_last = jnp.stack(
        [(last_rows[:, None] == (own_at + h * group)[None, :]) for h in range(2)]
    ).astype(BF16)

    near_scratch = pltpu.VMEM((WIDE, BLOCK), F32)
    held_scratch = [
        pltpu.VMEM((HELD, NBR, BLOCK, BLOCK), BF16),
        pltpu.SemaphoreType.DMA((HELD,)),
    ]
    pad_scratch = pltpu.VMEM((PAD, BLOCK), F32)
    msg_z = shape(Z, HELD * PAIR, BLOCK)
    held = shape(HELD * PAIR, BLOCK, dtype=F32)
    sums = shape(WIDE, BLOCK, dtype=F32)
    out = (msg_z, held, shape(HELD * PAD, BLOCK, dtype=F32))
    msg, solved, q = call(
        level1_kernel, out, "svv" + "h" * 7, [near_scratch] + held_scratch
    )(level, got, pick1, *ws)
    got = lax.all_to_all(msg, "z", 0, 0, tiled=True)
    msg, solved = call(
        level2_kernel, (msg_z, held), "svv" + "h" * 7 + "vv", [near_scratch] + held_scratch
    )(level, got, pick_z, *ws, q, solved)
    got = lax.all_to_all(msg, "z", 0, 0, tiled=True)
    msg, solved, before = call(
        level3_kernel,
        (msg_z, held, sums),
        "svv" + "h" * 7 + "vvv",
        [near_scratch, pad_scratch] + held_scratch,
    )(level, got, pick_z, *ws, q, solved, put_z)
    got = lax.all_to_all(msg, "z", 0, 0, tiled=True)
    msg, t, before = call(
        back2_kernel,
        (msg_z, held, sums),
        "sv" + "h" * 7 + "vvv",
        [near_scratch, pad_scratch] + held_scratch,
    )(level, got, *ws, solved, before, put_z)
    got = lax.all_to_all(msg, "z", 0, 0, tiled=True)
    msg, t = call(
        back1_kernel,
        (shape(Y * Z, 2 * group, BLOCK // 2), held),
        "sv" + "h" * 7 + "vvvv",
        [near_scratch, pad_scratch] + held_scratch,
    )(level, got, *ws, t, before, put_last, own_last)
    got = lax.all_to_all(msg, ROWS, 0, 0, tiled=True)
    mine = (my * Z + mz) * LOCAL + local_iota
    first = (rows_of(mine) < width).astype(jnp.int32)
    out = (shape(LOCAL, COUNT, BLOCK), shape(LOCAL, NBR + 1, BLOCK, BLOCK))
    column = jnp.arange(COUNT, dtype=jnp.int32)
    turn = (((column + PAIR * my) % COUNT)[:, None] == column[None, :]).astype(BF16)
    return call(final_kernel, out, "svvvvvvvvv")(
        first, got, q_own, probes, inverses, turn, *near_p
    )


def solution(mesh):
    fine = Mesh(mesh.devices.reshape(Y, Z, -1, 2), ("y", "z", "x", "c"))
    parts = ("x", "c")
    return jax.shard_map(
        body,
        mesh=fine,
        in_specs=(
            P(ROWS, parts, None),
            P(ROWS, None, None, None),
            P(ROWS, None, None),
            P(),
            P(),
        ),
        out_specs=(P(ROWS, parts, None), P(ROWS, parts, None, None)),
        check_vma=False,
    )
```

```python
import functools

import jax
import jax.numpy as jnp
from jax import lax
from jax.experimental import pallas as pl
from jax.experimental.pallas import tpu as pltpu
from jax.sharding import Mesh, PartitionSpec as P

LEVELS = 4
Y, Z = 4, 16
LOCAL, COUNT, BLOCK, NBR = 2, 8, 256, 4
PAIR = COUNT // Y
HELD = Y * LOCAL
PAD = 8
WIDE = HELD * NBR * PAD
ROWS = ("y", "z")
F32, BF16 = jnp.float32, jnp.bfloat16
NT = (((1,), (1,)), ((), ()))
TN = (((0,), (0,)), ((), ()))
VMEM = pl.BlockSpec(memory_space=pltpu.VMEM)
SMEM = pl.BlockSpec(memory_space=pltpu.SMEM)


def call(kernel, out_shape, places, scratch=(), room=52):
    kinds = {"s": SMEM, "v": VMEM, "h": pl.BlockSpec(memory_space=pl.ANY)}
    return pl.pallas_call(
        kernel,
        out_shape=out_shape,
        in_specs=[kinds[p] for p in places],
        out_specs=jax.tree.map(lambda _: VMEM, out_shape),
        scratch_shapes=list(scratch),
        compiler_params=pltpu.CompilerParams(vmem_limit_bytes=room * 2**20),
    )


def shape(*dims, dtype=BF16):
    return jax.ShapeDtypeStruct(dims, dtype)


def dot(a, b, dims=None):
    if dims is None:
        return jnp.dot(a, b, preferred_element_type=F32)
    return lax.dot_general(a, b, dims, preferred_element_type=F32)


def late(value):
    whole = pl.BlockSpec(memory_space=pltpu.HBM)
    return pl.pallas_call(
        lambda value_ref, same_ref: None,
        out_shape=shape(*value.shape),
        in_specs=[whole],
        out_specs=whole,
        input_output_aliases={0: 0},
        compiler_params=pltpu.CompilerParams(vmem_limit_bytes=52 * 2**20),
        cost_estimate=pl.CostEstimate(flops=20000000000, bytes_accessed=2**20, transcendentals=0),
    )(value)


def start_kernel(core_ref, probes_ref, inv_ref, factor_ref, q_ref, msg_ref, w_ref, send_ref, p_ref, d_ref, l_ref, sems):
    load_p = pltpu.make_async_copy(probes_ref, p_ref, sems.at[2])
    load_d = pltpu.make_async_copy(inv_ref, d_ref, sems.at[0])
    load_l = pltpu.make_async_copy(factor_ref, l_ref, sems.at[1])
    load_p.start()
    load_d.start()
    load_l.start()
    load_p.wait()
    load_d.wait()
    parts = []
    for s in range(LOCAL):
        q = dot(p_ref[s], d_ref[s], NT).astype(BF16)
        q_ref[s] = q
        parts.append(q.astype(F32))
    for s in range(LOCAL):
        parts.append(p_ref[s].astype(F32))
    for y in range(Y):
        msg = jnp.concatenate([p[y * PAIR : (y + 1) * PAIR] for p in parts], axis=0).astype(BF16)
        for z in range(Z):
            msg_ref[y * Z + z] = msg
    load_l.wait()
    for i in range(LOCAL):
        slot = (core_ref[0] + i) % LOCAL
        for k in range(NBR):
            w = dot(d_ref[slot], l_ref[slot, k]).astype(BF16)
            w_ref[i, k] = w
            if i == 0:
                send_ref[k] = w


def load_rows(level_ref, lev, w_refs, held_ref, sems):
    waits = []
    for r in range(HELD):
        d, slot = r // LOCAL, r % LOCAL
        source = w_refs[d].at[slot] if d < Y - 1 else w_refs[d + slot]
        copy = pltpu.make_async_copy(source, held_ref.at[r], sems.at[r])

        @pl.when(level_ref[r] == lev)
        def _():
            copy.start()

        waits.append(copy.wait)
    return waits


def forward_rows(level_ref, lev, waits, near_ref, q_ref, w_ref, solved_ref):
    for r in range(HELD):

        @pl.when(level_ref[r] == lev)
        def _():
            waits[r]()
            moved = jnp.zeros((PAD, BLOCK), F32)
            for k in range(NBR):
                at = (r * NBR + k) * PAD
                moved += dot(near_ref[at : at + PAD].astype(BF16), w_ref[r, k], NT)
            value = (q_ref[r * PAD : (r + 1) * PAD] - moved).astype(BF16).astype(F32)
            solved_ref[r * PAIR : (r + 1) * PAIR] = value[:PAIR]


def backward_rows(level_ref, lev, waits, t_ref, pad_ref, w_ref, terms_ref):
    terms_ref[...] = jnp.zeros_like(terms_ref)
    for r in range(HELD):

        @pl.when(level_ref[r] == lev)
        def _():
            if waits is not None:
                waits[r]()
            pad_ref[...] = jnp.zeros_like(pad_ref)
            pad_ref[:PAIR] = t_ref[r * PAIR : (r + 1) * PAIR]
            t = pad_ref[...].astype(BF16)
            for k in range(NBR):
                at = (r * NBR + k) * PAD
                terms_ref[at : at + PAD] = dot(t, w_ref[r, k])


def scatter(place, terms):
    high = terms.astype(BF16)
    low = (terms - high.astype(F32)).astype(BF16)
    return dot(place, high) + dot(place, low)


def broadcast_to_z(value, msg_ref):
    for z in range(Z):
        msg_ref[z] = value


def neighbour_kernel(got_ref, pick_ref, near_ref):
    got = got_ref[...].reshape(Y * Z * 4 * PAIR, BLOCK)
    near_ref[...] = dot(pick_ref[...], got).astype(BF16).reshape(near_ref.shape)


def level1_kernel(level_ref, got_ref, pick_ref, w0_ref, w1_ref, w2_ref, w3_ref, w4_ref, msg_ref, solved_ref, q_ref, near_ref, held_ref, sems):
    waits = load_rows(level_ref, 1, (w0_ref, w1_ref, w2_ref, w3_ref, w4_ref), held_ref, sems)
    got = got_ref[...].reshape(Y * Z * 4 * PAIR, BLOCK)
    near_ref[...] = dot(pick_ref[:WIDE], got)
    q_ref[...] = dot(pick_ref[WIDE : WIDE + HELD * PAD], got)
    for r in range(HELD):
        solved_ref[r * PAIR : (r + 1) * PAIR] = q_ref[r * PAD : r * PAD + PAIR]
    forward_rows(level_ref, 1, waits, near_ref, q_ref, held_ref, solved_ref)
    broadcast_to_z(solved_ref[...].astype(BF16), msg_ref)


def level2_kernel(level_ref, got_ref, pick_ref, w0_ref, w1_ref, w2_ref, w3_ref, w4_ref, q_ref, old_ref, _a, _b, _c, _d, msg_ref, solved_ref, near_ref, held_ref, sems):
    waits = load_rows(level_ref, 2, (w0_ref, w1_ref, w2_ref, w3_ref, w4_ref), held_ref, sems)
    near_ref[...] = dot(pick_ref[...], got_ref[...].reshape(Z * HELD * PAIR, BLOCK))
    solved_ref[...] = old_ref[...]
    forward_rows(level_ref, 2, waits, near_ref, q_ref, held_ref, solved_ref)
    broadcast_to_z(solved_ref[...].astype(BF16), msg_ref)


def level3_kernel(
    level_ref, got_ref, pick_ref, w0_ref, w1_ref, w2_ref, w3_ref, w4_ref, q_ref, old_ref, put_ref,
    msg_ref, solved_ref, terms_ref, near_ref, pad_ref, held_ref, sems):
    waits = load_rows(level_ref, 3, (w0_ref, w1_ref, w2_ref, w3_ref, w4_ref), held_ref, sems)
    near_ref[...] = dot(pick_ref[...], got_ref[...].reshape(Z * HELD * PAIR, BLOCK))
    solved_ref[...] = old_ref[...]
    forward_rows(level_ref, 3, waits, near_ref, q_ref, held_ref, solved_ref)
    backward_rows(level_ref, 3, None, solved_ref, pad_ref, held_ref, terms_ref)
    out = scatter(put_ref[...], terms_ref[...])
    msg_ref[...] = out.astype(BF16).reshape(msg_ref.shape)


def finish_rows(level_ref, lev, got_ref, old_ref, t_ref):
    acc = jnp.sum(got_ref[...].astype(F32), axis=0)
    t_ref[...] = old_ref[...]
    for r in range(HELD):

        @pl.when(level_ref[r] == lev)
        def _():
            rows = slice(r * PAIR, (r + 1) * PAIR)
            t_ref[rows] = (old_ref[rows] - acc[rows]).astype(BF16).astype(F32)


def back2_kernel(
    level_ref, got_ref, w0_ref, w1_ref, w2_ref, w3_ref, w4_ref, old_ref, before_ref, put_ref,
    msg_ref, t_ref, sums_ref, terms_ref, pad_ref, held_ref, sems):
    waits = load_rows(level_ref, 2, (w0_ref, w1_ref, w2_ref, w3_ref, w4_ref), held_ref, sems)
    finish_rows(level_ref, 2, got_ref, old_ref, t_ref)
    backward_rows(level_ref, 2, waits, t_ref, pad_ref, held_ref, terms_ref)
    sums_ref[...] = before_ref[...] + terms_ref[...]
    out = scatter(put_ref[...], sums_ref[...])
    msg_ref[...] = out.astype(BF16).reshape(msg_ref.shape)


def back1_kernel(
    level_ref, got_ref, w0_ref, w1_ref, w2_ref, w3_ref, w4_ref, old_ref, before_ref, put_ref, own_ref, msg_ref, t_ref, terms_ref, pad_ref, held_ref, sems):
    waits = load_rows(level_ref, 1, (w0_ref, w1_ref, w2_ref, w3_ref, w4_ref), held_ref, sems)
    finish_rows(level_ref, 1, got_ref, old_ref, t_ref)
    backward_rows(level_ref, 1, waits, t_ref, pad_ref, held_ref, terms_ref)
    sums = before_ref[...] + terms_ref[...]
    t = t_ref[...].astype(BF16)
    half = BLOCK // 2
    left = scatter(put_ref[0], sums[:, :half]) + dot(own_ref[0], t[:, :half])
    right = scatter(put_ref[1], sums[:, half:]) + dot(own_ref[1], t[:, half:])
    msg_ref[...] = (left + right).astype(BF16).reshape(msg_ref.shape)


def final_kernel(first_ref, got_ref, q_ref, probes_ref, inv_ref, turn_ref, near0_ref, near1_ref, near2_ref, near3_ref, x_ref, sel_ref):
    near_refs = (near0_ref, near1_ref, near2_ref, near3_ref)
    group = LOCAL * PAIR
    sums = []
    for y in range(Y):
        v = jnp.sum(got_ref[y * Z : (y + 1) * Z].astype(F32), axis=0)
        sums.append(jnp.concatenate([v[:group], v[group:]], axis=1))
    for s in range(LOCAL):
        acc = jnp.concatenate([v[s * PAIR : (s + 1) * PAIR] for v in sums], axis=0)
        base = jnp.where(first_ref[s] == 1, q_ref[s].astype(F32) - acc, acc)
        x = dot(base.astype(BF16), inv_ref[s]).astype(BF16)
        x_ref[s] = x
        turned = dot(turn_ref[...], x).astype(BF16)
        for k in range(NBR):
            at = (s * NBR + k) * PAIR
            near = jnp.concatenate(
                [ref[at : at + PAIR].astype(F32) for ref in near_refs], axis=0
            ).astype(BF16)
            sel_ref[s, k] = (dot(turned, near, TN) * (1.0 / COUNT)).astype(BF16)
        sel_ref[s, NBR] = (dot(x, probes_ref[s], TN) * (1.0 / COUNT)).astype(BF16)


def body(probes, factor, inverses, pattern, owner):
    my, mz = lax.axis_index("y"), lax.axis_index("z")
    total = owner.shape[0]
    width = total // LEVELS
    iota = jnp.arange(total, dtype=jnp.int32)

    core = lax.axis_index("c").reshape(1)
    w_shape = shape(NBR, BLOCK, BLOCK)
    w_pair = shape(LOCAL, NBR, BLOCK, BLOCK)
    out = (shape(LOCAL, COUNT, BLOCK), shape(Y * Z, 4 * PAIR, BLOCK), w_pair, w_shape)
    scratch = [
        pltpu.VMEM((LOCAL, COUNT, BLOCK), BF16),
        pltpu.VMEM((LOCAL, BLOCK, BLOCK), BF16),
        pltpu.VMEM((LOCAL, NBR, BLOCK, BLOCK), BF16),
        pltpu.SemaphoreType.DMA((3,)),
    ]
    q_own, msg, w_own, w_send = call(start_kernel, out, "shhh", scratch, room=60)(
        core, probes, inverses, factor
    )
    ring = [(2 * i, 2 * ((i + 1) % Y)) for i in range(Y)]
    ring += [(2 * i + 1, 2 * ((i - 1) % Y) + 1) for i in range(Y)]
    w_near = lax.ppermute(w_own, ("y", "c"), ring)
    w_far = lax.ppermute(w_send, "y", [(i, (i + 2) % Y) for i in range(Y)])
    got = lax.all_to_all(msg, ROWS, 0, 0, tiled=True)
    swap = [(0, 1), (1, 0)]
    ws = [w_own, w_near, late(lax.ppermute(w_near, "c", swap)), w_far, lax.ppermute(w_far, "c", swap)]

    def rows_of(slots):
        return jnp.sum(jnp.where(owner[None, :] == slots[:, None], iota[None, :], 0), axis=1)

    local_iota = jnp.arange(LOCAL, dtype=jnp.int32)
    way = 1 - 2 * lax.axis_index("c")
    held_y = (my + way * jnp.array([0, -1, 1, 2], jnp.int32)) % Y
    held_flip = jnp.array([0, 0, 1, 0], jnp.int32)
    core = lax.axis_index("c")
    flip = core + held_flip[:, None] + local_iota[None, :]
    slots = (LOCAL * (held_y * Z + mz))[:, None] + flip % LOCAL
    slots = slots.reshape(-1)
    rows = rows_of(slots)
    level = rows // width
    hit = rows[:, None, None] == iota[None, :, None]
    cols = jnp.sum(jnp.where(hit, pattern[None], 0), axis=1)
    src = jnp.sum(jnp.where(cols[..., None] == iota, owner, 0), axis=-1)
    src = jnp.where(cols >= 0, src, -1).reshape(-1)
    dev = src // LOCAL
    bad = -(2**20)
    turn = (way * (dev // Z - my)) % Y
    turn = jnp.where(turn == 3, 1, jnp.where(turn == 0, 0, turn + 1))
    place_z = jnp.where(src >= 0, (dev % Z) * HELD + turn * LOCAL + (src - core - (turn == 2)) % LOCAL, bad)

    def rows_at(place, pad, stride=PAIR):
        col = jnp.arange(pad, dtype=jnp.int32)
        at = jnp.where(col[None, :] < PAIR, place[:, None] * stride + col[None, :], bad)
        return at.reshape(-1)

    def hot(at, size):
        return (at[:, None] == jnp.arange(size, dtype=jnp.int32)[None, :]).astype(BF16)

    def first_at(slot, kind):
        return jnp.where(slot >= 0, (slot // LOCAL) * 4 + kind * LOCAL + slot % LOCAL, bad)

    natural = (((my - jnp.arange(Y, dtype=jnp.int32)) % Y)[:, None] * Z + mz) * LOCAL + local_iota[None, :]
    nat_rows = rows_of(natural.reshape(-1))
    nat_cols = jnp.sum(jnp.where(nat_rows[:, None, None] == iota[None, :, None], pattern[None], 0), axis=1)
    nat_src = jnp.sum(jnp.where(nat_cols[..., None] == iota, owner, 0), axis=-1)
    nat_src = jnp.where(nat_cols >= 0, nat_src, -1).reshape(-1)
    pick1 = jnp.concatenate(
        [
            rows_at(first_at(src, 0), PAD),
            rows_at(first_at(slots, 0), PAD),
        ]
    )
    pick1 = hot(pick1, Y * Z * 4 * PAIR)
    pick_p = hot(rows_at(first_at(nat_src, 1), PAIR), Y * Z * 4 * PAIR)
    near_p = call(neighbour_kernel, shape(Y, LOCAL * NBR * PAIR, BLOCK), "vv")(got, pick_p)
    near_p = [near_p[0]] + [
        lax.ppermute(near_p[d], "y", [(i, (i - d) % Y) for i in range(Y)]) for d in range(1, Y)
    ]
    at_z = rows_at(place_z, PAD)
    pick_z = hot(at_z, Z * HELD * PAIR)
    put_z = (jnp.arange(Z * HELD * PAIR, dtype=jnp.int32)[:, None] == at_z[None, :]).astype(BF16)
    level_of_src = jnp.where(cols >= 0, cols // width, LEVELS).reshape(-1)
    group = LOCAL * PAIR

    def last_at(slot, good):
        return jnp.where(good, (slot // LOCAL) * (2 * LOCAL) + slot % LOCAL, bad)

    size = Y * Z * 2 * group
    last_rows = jnp.arange(size, dtype=jnp.int32)
    put_at = rows_at(last_at(src, level_of_src == 0), PAD)
    own_at = rows_at(last_at(slots, level > 0), PAIR)
    put_last = jnp.stack(
        [(last_rows[:, None] == (put_at + h * group)[None, :]) for h in range(2)]
    ).astype(BF16)
    own_last = jnp.stack(
        [(last_rows[:, None] == (own_at + h * group)[None, :]) for h in range(2)]
    ).astype(BF16)

    near_scratch = pltpu.VMEM((WIDE, BLOCK), F32)
    held_scratch = [
        pltpu.VMEM((HELD, NBR, BLOCK, BLOCK), BF16),
        pltpu.SemaphoreType.DMA((HELD,)),
    ]
    pad_scratch = pltpu.VMEM((PAD, BLOCK), F32)
    msg_z = shape(Z, HELD * PAIR, BLOCK)
    held = shape(HELD * PAIR, BLOCK, dtype=F32)
    sums = shape(WIDE, BLOCK, dtype=F32)
    out = (msg_z, held, shape(HELD * PAD, BLOCK, dtype=F32))
    msg, solved, q = call(
        level1_kernel, out, "svv" + "h" * 5, [near_scratch] + held_scratch
    )(level, got, pick1, *ws)
    got = lax.all_to_all(msg, "z", 0, 0, tiled=True)
    msg, solved = call(
        level2_kernel, (msg_z, held), "svv" + "h" * 5 + "vvhhhh", [near_scratch] + held_scratch
    )(level, got, pick_z, *ws, q, solved, put_z, put_last, own_last, pick_p)
    got = lax.all_to_all(msg, "z", 0, 0, tiled=True)
    msg, solved, before = call(
        level3_kernel,
        (msg_z, held, sums),
        "svv" + "h" * 5 + "vvv",
        [near_scratch, pad_scratch] + held_scratch,
    )(level, got, pick_z, *ws, q, solved, put_z)
    got = lax.all_to_all(msg, "z", 0, 0, tiled=True)
    msg, t, before = call(
        back2_kernel,
        (msg_z, held, sums),
        "sv" + "h" * 5 + "vvv",
        [near_scratch, pad_scratch] + held_scratch,
    )(level, got, *ws, solved, before, put_z)
    got = lax.all_to_all(msg, "z", 0, 0, tiled=True)
    msg, t = call(
        back1_kernel,
        (shape(Y * Z, 2 * group, BLOCK // 2), held),
        "sv" + "h" * 5 + "vvvv",
        [near_scratch, pad_scratch] + held_scratch,
    )(level, got, *ws, t, before, put_last, own_last)
    got = lax.all_to_all(msg, ROWS, 0, 0, tiled=True)
    mine = (my * Z + mz) * LOCAL + local_iota
    first = (rows_of(mine) < width).astype(jnp.int32)
    out = (shape(LOCAL, COUNT, BLOCK), shape(LOCAL, NBR + 1, BLOCK, BLOCK))
    column = jnp.arange(COUNT, dtype=jnp.int32)
    turn = (((column + PAIR * my) % COUNT)[:, None] == column[None, :]).astype(BF16)
    return call(final_kernel, out, "svvvvvvvvv")(
        first, got, q_own, probes, inverses, turn, *near_p
    )


def solution(mesh):
    fine = Mesh(mesh.devices.reshape(Y, Z, -1, 2), ("y", "z", "x", "c"))
    parts = ("x", "c")
    return jax.shard_map(
        body,
        mesh=fine,
        in_specs=(
            P(ROWS, parts, None),
            P(ROWS, None, None, None),
            P(ROWS, None, None),
            P(),
            P(),
        ),
        out_specs=(P(ROWS, parts, None), P(ROWS, parts, None, None)),
        check_vma=False,
    )
```

```python
import functools

import jax
import jax.numpy as jnp
from jax import lax
from jax.experimental import pallas as pl
from jax.experimental.pallas import tpu as pltpu
from jax.sharding import Mesh, PartitionSpec as P

LEVELS = 4
Y, Z = 4, 16
LOCAL, COUNT, BLOCK, NBR = 2, 8, 256, 4
PAIR = COUNT // Y
HELD = Y * LOCAL
PAD = 8
WIDE = HELD * NBR * PAD
ROWS = ("y", "z")
F32, BF16 = jnp.float32, jnp.bfloat16
NT = (((1,), (1,)), ((), ()))
TN = (((0,), (0,)), ((), ()))
VMEM = pl.BlockSpec(memory_space=pltpu.VMEM)
SMEM = pl.BlockSpec(memory_space=pltpu.SMEM)


def call(kernel, out_shape, places, scratch=(), room=52):
    kinds = {"s": SMEM, "v": VMEM, "h": pl.BlockSpec(memory_space=pl.ANY)}
    return pl.pallas_call(
        kernel,
        out_shape=out_shape,
        in_specs=[kinds[p] for p in places],
        out_specs=jax.tree.map(lambda _: VMEM, out_shape),
        scratch_shapes=list(scratch),
        compiler_params=pltpu.CompilerParams(vmem_limit_bytes=room * 2**20),
    )


def shape(*dims, dtype=BF16):
    return jax.ShapeDtypeStruct(dims, dtype)


def dot(a, b, dims=None):
    if dims is None:
        return jnp.dot(a, b, preferred_element_type=F32)
    return lax.dot_general(a, b, dims, preferred_element_type=F32)


def late(value):
    whole = pl.BlockSpec(memory_space=pltpu.HBM)
    return pl.pallas_call(
        lambda value_ref, same_ref: None,
        out_shape=shape(*value.shape),
        in_specs=[whole],
        out_specs=whole,
        input_output_aliases={0: 0},
        compiler_params=pltpu.CompilerParams(vmem_limit_bytes=52 * 2**20),
        cost_estimate=pl.CostEstimate(flops=20000000000, bytes_accessed=2**20, transcendentals=0),
    )(value)


def start_kernel(core_ref, probes_ref, inv_ref, factor_ref, q_ref, msg_ref, w_ref, send_ref, p_ref, d_ref, l_ref, sems):
    load_p = pltpu.make_async_copy(probes_ref, p_ref, sems.at[2])
    load_d = pltpu.make_async_copy(inv_ref, d_ref, sems.at[0])
    load_l = pltpu.make_async_copy(factor_ref, l_ref, sems.at[1])
    load_p.start()
    load_d.start()
    load_l.start()
    load_p.wait()
    load_d.wait()
    parts = []
    for s in range(LOCAL):
        q = dot(p_ref[s], d_ref[s], NT).astype(BF16)
        q_ref[s] = q
        parts.append(q.astype(F32))
    for s in range(LOCAL):
        parts.append(p_ref[s].astype(F32))
    for y in range(Y):
        msg = jnp.concatenate([p[y * PAIR : (y + 1) * PAIR] for p in parts], axis=0).astype(BF16)
        for z in range(Z):
            msg_ref[y * Z + z] = msg
    load_l.wait()
    for i in range(LOCAL):
        slot = (core_ref[0] + i) % LOCAL
        for k in range(NBR):
            w = dot(d_ref[slot], l_ref[slot, k]).astype(BF16)
            w_ref[i, k] = w
            if i == 0:
                send_ref[k] = w


def load_rows(level_ref, lev, w_refs, held_ref, sems):
    waits = []
    for r in range(HELD):
        d, slot = r // LOCAL, r % LOCAL
        source = w_refs[d].at[slot] if d < Y - 1 else w_refs[d + slot]
        copy = pltpu.make_async_copy(source, held_ref.at[r], sems.at[r])

        @pl.when(level_ref[r] == lev)
        def _():
            copy.start()

        waits.append(copy.wait)
    return waits


def forward_rows(level_ref, lev, waits, near_ref, q_ref, w_ref, solved_ref):
    for r in range(HELD):

        @pl.when(level_ref[r] == lev)
        def _():
            waits[r]()
            moved = jnp.zeros((PAD, BLOCK), F32)
            for k in range(NBR):
                at = (r * NBR + k) * PAD
                moved += dot(near_ref[at : at + PAD].astype(BF16), w_ref[r, k], NT)
            value = (q_ref[r * PAD : (r + 1) * PAD] - moved).astype(BF16).astype(F32)
            solved_ref[r * PAIR : (r + 1) * PAIR] = value[:PAIR]


def backward_rows(level_ref, lev, waits, t_ref, pad_ref, w_ref, terms_ref):
    terms_ref[...] = jnp.zeros_like(terms_ref)
    for r in range(HELD):

        @pl.when(level_ref[r] == lev)
        def _():
            if waits is not None:
                waits[r]()
            pad_ref[...] = jnp.zeros_like(pad_ref)
            pad_ref[:PAIR] = t_ref[r * PAIR : (r + 1) * PAIR]
            t = pad_ref[...].astype(BF16)
            for k in range(NBR):
                at = (r * NBR + k) * PAD
                terms_ref[at : at + PAD] = dot(t, w_ref[r, k])


def scatter(place, terms):
    high = terms.astype(BF16)
    low = (terms - high.astype(F32)).astype(BF16)
    return dot(place, high) + dot(place, low)


def broadcast_to_z(value, msg_ref):
    for z in range(Z):
        msg_ref[z] = value


def neighbour_kernel(got_ref, pick_ref, _, near_ref):
    got = got_ref[...].reshape(Y * Z * 4 * PAIR, BLOCK)
    near_ref[...] = dot(pick_ref[...], got).astype(BF16)


def level1_kernel(level_ref, got_ref, pick_ref, w0_ref, w1_ref, w2_ref, w3_ref, w4_ref, msg_ref, solved_ref, q_ref, near_ref, held_ref, sems):
    waits = load_rows(level_ref, 1, (w0_ref, w1_ref, w2_ref, w3_ref, w4_ref), held_ref, sems)
    got = got_ref[...].reshape(Y * Z * 4 * PAIR, BLOCK)
    near_ref[...] = dot(pick_ref[:WIDE], got)
    q_ref[...] = dot(pick_ref[WIDE : WIDE + HELD * PAD], got)
    for r in range(HELD):
        solved_ref[r * PAIR : (r + 1) * PAIR] = q_ref[r * PAD : r * PAD + PAIR]
    forward_rows(level_ref, 1, waits, near_ref, q_ref, held_ref, solved_ref)
    broadcast_to_z(solved_ref[...].astype(BF16), msg_ref)


def level2_kernel(level_ref, got_ref, pick_ref, w0_ref, w1_ref, w2_ref, w3_ref, w4_ref, q_ref, old_ref, _a, _b, _c, _d, msg_ref, solved_ref, near_ref, held_ref, sems):
    waits = load_rows(level_ref, 2, (w0_ref, w1_ref, w2_ref, w3_ref, w4_ref), held_ref, sems)
    near_ref[...] = dot(pick_ref[...], got_ref[...].reshape(Z * HELD * PAIR, BLOCK))
    solved_ref[...] = old_ref[...]
    forward_rows(level_ref, 2, waits, near_ref, q_ref, held_ref, solved_ref)
    broadcast_to_z(solved_ref[...].astype(BF16), msg_ref)


def level3_kernel(
    level_ref, got_ref, pick_ref, w0_ref, w1_ref, w2_ref, w3_ref, w4_ref, q_ref, old_ref, put_ref,
    msg_ref, solved_ref, terms_ref, near_ref, pad_ref, held_ref, sems):
    waits = load_rows(level_ref, 3, (w0_ref, w1_ref, w2_ref, w3_ref, w4_ref), held_ref, sems)
    near_ref[...] = dot(pick_ref[...], got_ref[...].reshape(Z * HELD * PAIR, BLOCK))
    solved_ref[...] = old_ref[...]
    forward_rows(level_ref, 3, waits, near_ref, q_ref, held_ref, solved_ref)
    backward_rows(level_ref, 3, None, solved_ref, pad_ref, held_ref, terms_ref)
    out = scatter(put_ref[...], terms_ref[...])
    msg_ref[...] = out.astype(BF16).reshape(msg_ref.shape)


def finish_rows(level_ref, lev, got_ref, old_ref, t_ref):
    acc = jnp.sum(got_ref[...].astype(F32), axis=0)
    t_ref[...] = old_ref[...]
    for r in range(HELD):

        @pl.when(level_ref[r] == lev)
        def _():
            rows = slice(r * PAIR, (r + 1) * PAIR)
            t_ref[rows] = (old_ref[rows] - acc[rows]).astype(BF16).astype(F32)


def back2_kernel(
    level_ref, got_ref, w0_ref, w1_ref, w2_ref, w3_ref, w4_ref, old_ref, before_ref, put_ref,
    msg_ref, t_ref, sums_ref, terms_ref, pad_ref, held_ref, sems):
    waits = load_rows(level_ref, 2, (w0_ref, w1_ref, w2_ref, w3_ref, w4_ref), held_ref, sems)
    finish_rows(level_ref, 2, got_ref, old_ref, t_ref)
    backward_rows(level_ref, 2, waits, t_ref, pad_ref, held_ref, terms_ref)
    sums_ref[...] = before_ref[...] + terms_ref[...]
    out = scatter(put_ref[...], sums_ref[...])
    msg_ref[...] = out.astype(BF16).reshape(msg_ref.shape)


def back1_kernel(
    level_ref, got_ref, w0_ref, w1_ref, w2_ref, w3_ref, w4_ref, old_ref, before_ref, put_ref, own_ref, msg_ref, t_ref, terms_ref, pad_ref, held_ref, sems):
    waits = load_rows(level_ref, 1, (w0_ref, w1_ref, w2_ref, w3_ref, w4_ref), held_ref, sems)
    finish_rows(level_ref, 1, got_ref, old_ref, t_ref)
    backward_rows(level_ref, 1, waits, t_ref, pad_ref, held_ref, terms_ref)
    sums = before_ref[...] + terms_ref[...]
    t = t_ref[...].astype(BF16)
    half = BLOCK // 2
    left = scatter(put_ref[0], sums[:, :half]) + dot(own_ref[0], t[:, :half])
    right = scatter(put_ref[1], sums[:, half:]) + dot(own_ref[1], t[:, half:])
    msg_ref[...] = (left + right).astype(BF16).reshape(msg_ref.shape)


def final_kernel(first_ref, got_ref, q_ref, probes_ref, inv_ref, turn_ref, near0_ref, near1_ref, near2_ref, near3_ref, x_ref, sel_ref):
    near_refs = (near0_ref, near1_ref, near2_ref, near3_ref)
    group = LOCAL * PAIR
    sums = []
    for y in range(Y):
        v = jnp.sum(got_ref[y * Z : (y + 1) * Z].astype(F32), axis=0)
        sums.append(jnp.concatenate([v[:group], v[group:]], axis=1))
    for s in range(LOCAL):
        acc = jnp.concatenate([v[s * PAIR : (s + 1) * PAIR] for v in sums], axis=0)
        base = jnp.where(first_ref[s] == 1, q_ref[s].astype(F32) - acc, acc)
        x = dot(base.astype(BF16), inv_ref[s]).astype(BF16)
        x_ref[s] = x
        turned = dot(turn_ref[...], x).astype(BF16)
        for k in range(NBR):
            at = (s * NBR + k) * PAIR
            near = jnp.concatenate(
                [ref[at : at + PAIR].astype(F32) for ref in near_refs], axis=0
            ).astype(BF16)
            sel_ref[s, k] = (dot(turned, near, TN) * (1.0 / COUNT)).astype(BF16)
        sel_ref[s, NBR] = (dot(x, probes_ref[s], TN) * (1.0 / COUNT)).astype(BF16)


def body(probes, factor, inverses, pattern, owner):
    my, mz = lax.axis_index("y"), lax.axis_index("z")
    total = owner.shape[0]
    width = total // LEVELS
    iota = jnp.arange(total, dtype=jnp.int32)

    core = lax.axis_index("c").reshape(1)
    w_shape = shape(NBR, BLOCK, BLOCK)
    w_pair = shape(LOCAL, NBR, BLOCK, BLOCK)
    out = (shape(LOCAL, COUNT, BLOCK), shape(Y * Z, 4 * PAIR, BLOCK), w_pair, w_shape)
    scratch = [
        pltpu.VMEM((LOCAL, COUNT, BLOCK), BF16),
        pltpu.VMEM((LOCAL, BLOCK, BLOCK), BF16),
        pltpu.VMEM((LOCAL, NBR, BLOCK, BLOCK), BF16),
        pltpu.SemaphoreType.DMA((3,)),
    ]
    q_own, msg, w_own, w_send = call(start_kernel, out, "shhh", scratch, room=60)(
        core, probes, inverses, factor
    )
    ring = [(2 * i, 2 * ((i + 1) % Y)) for i in range(Y)]
    ring += [(2 * i + 1, 2 * ((i - 1) % Y) + 1) for i in range(Y)]
    w_near = lax.ppermute(w_own, ("y", "c"), ring)
    w_far = lax.ppermute(w_send, "y", [(i, (i + 2) % Y) for i in range(Y)])
    got = lax.all_to_all(msg, ROWS, 0, 0, tiled=True)
    swap = [(0, 1), (1, 0)]
    ws = [w_own, w_near, late(lax.ppermute(w_near, "c", swap)), w_far, lax.ppermute(w_far, "c", swap)]

    def rows_of(slots):
        return jnp.sum(jnp.where(owner[None, :] == slots[:, None], iota[None, :], 0), axis=1)

    local_iota = jnp.arange(LOCAL, dtype=jnp.int32)
    way = 1 - 2 * lax.axis_index("c")
    held_y = (my + way * jnp.array([0, -1, 1, 2], jnp.int32)) % Y
    held_flip = jnp.array([0, 0, 1, 0], jnp.int32)
    core = lax.axis_index("c")
    flip = core + held_flip[:, None] + local_iota[None, :]
    slots = (LOCAL * (held_y * Z + mz))[:, None] + flip % LOCAL
    slots = slots.reshape(-1)
    rows = rows_of(slots)
    level = rows // width
    hit = rows[:, None, None] == iota[None, :, None]
    cols = jnp.sum(jnp.where(hit, pattern[None], 0), axis=1)
    src = jnp.sum(jnp.where(cols[..., None] == iota, owner, 0), axis=-1)
    src = jnp.where(cols >= 0, src, -1).reshape(-1)
    dev = src // LOCAL
    bad = -(2**20)
    turn = (way * (dev // Z - my)) % Y
    turn = jnp.where(turn == 3, 1, jnp.where(turn == 0, 0, turn + 1))
    place_z = jnp.where(src >= 0, (dev % Z) * HELD + turn * LOCAL + (src - core - (turn == 2)) % LOCAL, bad)

    def rows_at(place, pad, stride=PAIR):
        col = jnp.arange(pad, dtype=jnp.int32)
        at = jnp.where(col[None, :] < PAIR, place[:, None] * stride + col[None, :], bad)
        return at.reshape(-1)

    def hot(at, size):
        return (at[:, None] == jnp.arange(size, dtype=jnp.int32)[None, :]).astype(BF16)

    def first_at(slot, kind):
        return jnp.where(slot >= 0, (slot // LOCAL) * 4 + kind * LOCAL + slot % LOCAL, bad)

    natural = (((my - jnp.arange(Y, dtype=jnp.int32)) % Y)[:, None] * Z + mz) * LOCAL + local_iota[None, :]
    nat_rows = rows_of(natural.reshape(-1))
    nat_cols = jnp.sum(jnp.where(nat_rows[:, None, None] == iota[None, :, None], pattern[None], 0), axis=1)
    nat_src = jnp.sum(jnp.where(nat_cols[..., None] == iota, owner, 0), axis=-1)
    nat_src = jnp.where(nat_cols >= 0, nat_src, -1).reshape(-1)
    pick1 = jnp.concatenate(
        [
            rows_at(first_at(src, 0), PAD),
            rows_at(first_at(slots, 0), PAD),
        ]
    )
    pick1 = hot(pick1, Y * Z * 4 * PAIR)
    pick_p = hot(rows_at(first_at(nat_src, 1), PAIR), Y * Z * 4 * PAIR)
    got_first = got

    def neighbours(d, since):
        rows = LOCAL * NBR * PAIR
        near = call(neighbour_kernel, shape(rows, BLOCK), "vvh")(
            got_first, pick_p[d * rows : (d + 1) * rows], since
        )
        return lax.ppermute(near, "y", [(i, (i - d) % Y) for i in range(Y)]) if d else near

    at_z = rows_at(place_z, PAD)
    pick_z = hot(at_z, Z * HELD * PAIR)
    put_z = (jnp.arange(Z * HELD * PAIR, dtype=jnp.int32)[:, None] == at_z[None, :]).astype(BF16)
    level_of_src = jnp.where(cols >= 0, cols // width, LEVELS).reshape(-1)
    group = LOCAL * PAIR

    def last_at(slot, good):
        return jnp.where(good, (slot // LOCAL) * (2 * LOCAL) + slot % LOCAL, bad)

    size = Y * Z * 2 * group
    last_rows = jnp.arange(size, dtype=jnp.int32)
    put_at = rows_at(last_at(src, level_of_src == 0), PAD)
    own_at = rows_at(last_at(slots, level > 0), PAIR)
    put_last = jnp.stack(
        [(last_rows[:, None] == (put_at + h * group)[None, :]) for h in range(2)]
    ).astype(BF16)
    own_last = jnp.stack(
        [(last_rows[:, None] == (own_at + h * group)[None, :]) for h in range(2)]
    ).astype(BF16)

    near_scratch = pltpu.VMEM((WIDE, BLOCK), F32)
    held_scratch = [
        pltpu.VMEM((HELD, NBR, BLOCK, BLOCK), BF16),
        pltpu.SemaphoreType.DMA((HELD,)),
    ]
    pad_scratch = pltpu.VMEM((PAD, BLOCK), F32)
    msg_z = shape(Z, HELD * PAIR, BLOCK)
    held = shape(HELD * PAIR, BLOCK, dtype=F32)
    sums = shape(WIDE, BLOCK, dtype=F32)
    out = (msg_z, held, shape(HELD * PAD, BLOCK, dtype=F32))
    msg, solved, q = call(
        level1_kernel, out, "svv" + "h" * 5, [near_scratch] + held_scratch
    )(level, got, pick1, *ws)
    got = lax.all_to_all(msg, "z", 0, 0, tiled=True)
    near1 = neighbours(1, solved)
    msg, solved = call(
        level2_kernel, (msg_z, held), "svv" + "h" * 5 + "vvhhhh", [near_scratch] + held_scratch
    )(level, got, pick_z, *ws, q, solved, put_z, put_last, own_last, near1)
    got = lax.all_to_all(msg, "z", 0, 0, tiled=True)
    msg, solved, before = call(
        level3_kernel,
        (msg_z, held, sums),
        "svv" + "h" * 5 + "vvv",
        [near_scratch, pad_scratch] + held_scratch,
    )(level, got, pick_z, *ws, q, solved, put_z)
    got = lax.all_to_all(msg, "z", 0, 0, tiled=True)
    msg, t, before = call(
        back2_kernel,
        (msg_z, held, sums),
        "sv" + "h" * 5 + "vvv",
        [near_scratch, pad_scratch] + held_scratch,
    )(level, got, *ws, solved, before, put_z)
    got = lax.all_to_all(msg, "z", 0, 0, tiled=True)
    msg, t = call(
        back1_kernel,
        (shape(Y * Z, 2 * group, BLOCK // 2), held),
        "sv" + "h" * 5 + "vvvv",
        [near_scratch, pad_scratch] + held_scratch,
    )(level, got, *ws, t, before, put_last, own_last)
    got = lax.all_to_all(msg, ROWS, 0, 0, tiled=True)
    mine = (my * Z + mz) * LOCAL + local_iota
    first = (rows_of(mine) < width).astype(jnp.int32)
    out = (shape(LOCAL, COUNT, BLOCK), shape(LOCAL, NBR + 1, BLOCK, BLOCK))
    column = jnp.arange(COUNT, dtype=jnp.int32)
    turn = (((column + PAIR * my) % COUNT)[:, None] == column[None, :]).astype(BF16)
    return call(final_kernel, out, "svvvvvvvvv")(
        first, got, q_own, probes, inverses, turn, neighbours(0, t), near1, neighbours(2, t), neighbours(3, t)
    )


def solution(mesh):
    fine = Mesh(mesh.devices.reshape(Y, Z, -1, 2), ("y", "z", "x", "c"))
    parts = ("x", "c")
    return jax.shard_map(
        body,
        mesh=fine,
        in_specs=(
            P(ROWS, parts, None),
            P(ROWS, None, None, None),
            P(ROWS, None, None),
            P(),
            P(),
        ),
        out_specs=(P(ROWS, parts, None), P(ROWS, parts, None, None)),
        check_vma=False,
    )
```

```python
import functools

import jax
import jax.numpy as jnp
from jax import lax
from jax.experimental import pallas as pl
from jax.experimental.pallas import tpu as pltpu
from jax.sharding import Mesh, PartitionSpec as P

LEVELS = 4
Y, Z = 4, 16
LOCAL, COUNT, BLOCK, NBR = 2, 8, 256, 4
PAIR = COUNT // Y
HELD = Y * LOCAL
PAD = 8
WIDE = HELD * NBR * PAD
ROWS = ("y", "z")
F32, BF16 = jnp.float32, jnp.bfloat16
NT = (((1,), (1,)), ((), ()))
TN = (((0,), (0,)), ((), ()))
VMEM = pl.BlockSpec(memory_space=pltpu.VMEM)
SMEM = pl.BlockSpec(memory_space=pltpu.SMEM)


def call(kernel, out_shape, places, scratch=(), room=52):
    kinds = {"s": SMEM, "v": VMEM, "h": pl.BlockSpec(memory_space=pl.ANY)}
    return pl.pallas_call(
        kernel,
        out_shape=out_shape,
        in_specs=[kinds[p] for p in places],
        out_specs=jax.tree.map(lambda _: VMEM, out_shape),
        scratch_shapes=list(scratch),
        compiler_params=pltpu.CompilerParams(vmem_limit_bytes=room * 2**20),
    )


def shape(*dims, dtype=BF16):
    return jax.ShapeDtypeStruct(dims, dtype)


def dot(a, b, dims=None):
    if dims is None:
        return jnp.dot(a, b, preferred_element_type=F32)
    return lax.dot_general(a, b, dims, preferred_element_type=F32)


def late(value):
    whole = pl.BlockSpec(memory_space=pltpu.HBM)
    return pl.pallas_call(
        lambda value_ref, same_ref: None,
        out_shape=shape(*value.shape),
        in_specs=[whole],
        out_specs=whole,
        input_output_aliases={0: 0},
        compiler_params=pltpu.CompilerParams(vmem_limit_bytes=52 * 2**20),
        cost_estimate=pl.CostEstimate(flops=20000000000, bytes_accessed=2**20, transcendentals=0),
    )(value)


def start_kernel(core_ref, probes_ref, inv_ref, factor_ref, q_ref, msg_ref, w_ref, send_ref, p_ref, d_ref, l_ref, sems):
    load_p = pltpu.make_async_copy(probes_ref, p_ref, sems.at[2])
    load_d = pltpu.make_async_copy(inv_ref, d_ref, sems.at[0])
    load_l = pltpu.make_async_copy(factor_ref, l_ref, sems.at[1])
    load_p.start()
    load_d.start()
    load_l.start()
    load_p.wait()
    load_d.wait()
    parts = []
    for s in range(LOCAL):
        q = dot(p_ref[s], d_ref[s], NT).astype(BF16)
        q_ref[s] = q
        parts.append(q.astype(F32))
    for s in range(LOCAL):
        parts.append(p_ref[s].astype(F32))
    for y in range(Y):
        msg = jnp.concatenate([p[y * PAIR : (y + 1) * PAIR] for p in parts], axis=0).astype(BF16)
        for z in range(Z):
            msg_ref[y * Z + z] = msg
    load_l.wait()
    for i in range(LOCAL):
        slot = (core_ref[0] + i) % LOCAL
        for k in range(NBR):
            w = dot(d_ref[slot], l_ref[slot, k]).astype(BF16)
            w_ref[i, k] = w
            if i == 0:
                send_ref[k] = w


def load_rows(level_ref, lev, w_refs, held_ref, sems):
    waits = []
    for r in range(HELD):
        d, slot = r // LOCAL, r % LOCAL
        source = w_refs[d].at[slot] if d < Y - 1 else w_refs[d + slot]
        copy = pltpu.make_async_copy(source, held_ref.at[r], sems.at[r])

        @pl.when(level_ref[r] == lev)
        def _():
            copy.start()

        waits.append(copy.wait)
    return waits


def forward_rows(level_ref, lev, waits, near_ref, q_ref, w_ref, solved_ref):
    for r in range(HELD):

        @pl.when(level_ref[r] == lev)
        def _():
            waits[r]()
            moved = jnp.zeros((PAD, BLOCK), F32)
            for k in range(NBR):
                at = (r * NBR + k) * PAD
                moved += dot(near_ref[at : at + PAD].astype(BF16), w_ref[r, k], NT)
            value = (q_ref[r * PAD : (r + 1) * PAD] - moved).astype(BF16).astype(F32)
            solved_ref[r * PAIR : (r + 1) * PAIR] = value[:PAIR]


def backward_rows(level_ref, lev, waits, t_ref, pad_ref, w_ref, terms_ref):
    terms_ref[...] = jnp.zeros_like(terms_ref)
    for r in range(HELD):

        @pl.when(level_ref[r] == lev)
        def _():
            if waits is not None:
                waits[r]()
            pad_ref[...] = jnp.zeros_like(pad_ref)
            pad_ref[:PAIR] = t_ref[r * PAIR : (r + 1) * PAIR]
            t = pad_ref[...].astype(BF16)
            for k in range(NBR):
                at = (r * NBR + k) * PAD
                terms_ref[at : at + PAD] = dot(t, w_ref[r, k])


def scatter(place, terms):
    high = terms.astype(BF16)
    low = (terms - high.astype(F32)).astype(BF16)
    return dot(place, high) + dot(place, low)


def broadcast_to_z(value, msg_ref):
    for z in range(Z):
        msg_ref[z] = value


def neighbour_kernel(got_ref, pick_ref, _, near_ref):
    got = got_ref[...].reshape(Y * Z * 4 * PAIR, BLOCK)
    near_ref[...] = dot(pick_ref[...], got).astype(BF16)


def level1_kernel(level_ref, got_ref, pick_ref, w0_ref, w1_ref, w2_ref, w3_ref, w4_ref, msg_ref, solved_ref, q_ref, near_ref, held_ref, sems):
    waits = load_rows(level_ref, 1, (w0_ref, w1_ref, w2_ref, w3_ref, w4_ref), held_ref, sems)
    got = got_ref[...].reshape(Y * Z * 4 * PAIR, BLOCK)
    near_ref[...] = dot(pick_ref[:WIDE], got)
    q_ref[...] = dot(pick_ref[WIDE : WIDE + HELD * PAD], got)
    for r in range(HELD):
        solved_ref[r * PAIR : (r + 1) * PAIR] = q_ref[r * PAD : r * PAD + PAIR]
    forward_rows(level_ref, 1, waits, near_ref, q_ref, held_ref, solved_ref)
    broadcast_to_z(solved_ref[...].astype(BF16), msg_ref)


def level2_kernel(level_ref, got_ref, pick_ref, w0_ref, w1_ref, w2_ref, w3_ref, w4_ref, q_ref, old_ref, _a, _b, _c, _d, msg_ref, solved_ref, near_ref, held_ref, sems):
    waits = load_rows(level_ref, 2, (w0_ref, w1_ref, w2_ref, w3_ref, w4_ref), held_ref, sems)
    near_ref[...] = dot(pick_ref[...], got_ref[...].reshape(Z * HELD * PAIR, BLOCK))
    solved_ref[...] = old_ref[...]
    forward_rows(level_ref, 2, waits, near_ref, q_ref, held_ref, solved_ref)
    broadcast_to_z(solved_ref[...].astype(BF16), msg_ref)


def level3_kernel(
    level_ref, got_ref, pick_ref, w0_ref, w1_ref, w2_ref, w3_ref, w4_ref, q_ref, old_ref, put_ref,
    msg_ref, solved_ref, terms_ref, near_ref, pad_ref, held_ref, sems):
    waits = load_rows(level_ref, 3, (w0_ref, w1_ref, w2_ref, w3_ref, w4_ref), held_ref, sems)
    near_ref[...] = dot(pick_ref[...], got_ref[...].reshape(Z * HELD * PAIR, BLOCK))
    solved_ref[...] = old_ref[...]
    forward_rows(level_ref, 3, waits, near_ref, q_ref, held_ref, solved_ref)
    backward_rows(level_ref, 3, None, solved_ref, pad_ref, held_ref, terms_ref)
    out = scatter(put_ref[...], terms_ref[...])
    msg_ref[...] = out.astype(BF16).reshape(msg_ref.shape)


def finish_rows(level_ref, lev, got_ref, old_ref, t_ref):
    acc = jnp.sum(got_ref[...].astype(F32), axis=0)
    t_ref[...] = old_ref[...]
    for r in range(HELD):

        @pl.when(level_ref[r] == lev)
        def _():
            rows = slice(r * PAIR, (r + 1) * PAIR)
            t_ref[rows] = (old_ref[rows] - acc[rows]).astype(BF16).astype(F32)


def back2_kernel(
    level_ref, got_ref, w0_ref, w1_ref, w2_ref, w3_ref, w4_ref, old_ref, before_ref, put_ref,
    msg_ref, t_ref, sums_ref, terms_ref, pad_ref, held_ref, sems):
    waits = load_rows(level_ref, 2, (w0_ref, w1_ref, w2_ref, w3_ref, w4_ref), held_ref, sems)
    finish_rows(level_ref, 2, got_ref, old_ref, t_ref)
    backward_rows(level_ref, 2, waits, t_ref, pad_ref, held_ref, terms_ref)
    sums_ref[...] = before_ref[...] + terms_ref[...]
    out = scatter(put_ref[...], sums_ref[...])
    msg_ref[...] = out.astype(BF16).reshape(msg_ref.shape)


def back1_kernel(
    level_ref, got_ref, w0_ref, w1_ref, w2_ref, w3_ref, w4_ref, old_ref, before_ref, put_ref, own_ref, msg_ref, t_ref, terms_ref, pad_ref, held_ref, sems):
    waits = load_rows(level_ref, 1, (w0_ref, w1_ref, w2_ref, w3_ref, w4_ref), held_ref, sems)
    finish_rows(level_ref, 1, got_ref, old_ref, t_ref)
    backward_rows(level_ref, 1, waits, t_ref, pad_ref, held_ref, terms_ref)
    sums = before_ref[...] + terms_ref[...]
    t = t_ref[...].astype(BF16)
    half = BLOCK // 2
    group = LOCAL * PAIR
    size = Y * Z * 2 * group

    def hot(at, h):
        rows = lax.broadcasted_iota(jnp.int32, (size, at.shape[1]), 0)
        return jnp.where(rows == at + h * group, 1.0, 0.0).astype(BF16)

    put_at, own_at = put_ref[...], own_ref[...]
    left = scatter(hot(put_at, 0), sums[:, :half]) + dot(hot(own_at, 0), t[:, :half])
    right = scatter(hot(put_at, 1), sums[:, half:]) + dot(hot(own_at, 1), t[:, half:])
    msg_ref[...] = (left + right).astype(BF16).reshape(msg_ref.shape)


def final_kernel(first_ref, got_ref, q_ref, probes_ref, inv_ref, turn_ref, near0_ref, near1_ref, near2_ref, near3_ref, x_ref, sel_ref):
    near_refs = (near0_ref, near1_ref, near2_ref, near3_ref)
    group = LOCAL * PAIR
    sums = []
    for y in range(Y):
        v = jnp.sum(got_ref[y * Z : (y + 1) * Z].astype(F32), axis=0)
        sums.append(jnp.concatenate([v[:group], v[group:]], axis=1))
    for s in range(LOCAL):
        acc = jnp.concatenate([v[s * PAIR : (s + 1) * PAIR] for v in sums], axis=0)
        base = jnp.where(first_ref[s] == 1, q_ref[s].astype(F32) - acc, acc)
        x = dot(base.astype(BF16), inv_ref[s]).astype(BF16)
        x_ref[s] = x
        turned = dot(turn_ref[...], x).astype(BF16)
        for k in range(NBR):
            at = (s * NBR + k) * PAIR
            near = jnp.concatenate(
                [ref[at : at + PAIR].astype(F32) for ref in near_refs], axis=0
            ).astype(BF16)
            sel_ref[s, k] = (dot(turned, near, TN) * (1.0 / COUNT)).astype(BF16)
        sel_ref[s, NBR] = (dot(x, probes_ref[s], TN) * (1.0 / COUNT)).astype(BF16)


def body(probes, factor, inverses, pattern, owner):
    my, mz = lax.axis_index("y"), lax.axis_index("z")
    total = owner.shape[0]
    width = total // LEVELS
    iota = jnp.arange(total, dtype=jnp.int32)

    core = lax.axis_index("c").reshape(1)
    w_shape = shape(NBR, BLOCK, BLOCK)
    w_pair = shape(LOCAL, NBR, BLOCK, BLOCK)
    out = (shape(LOCAL, COUNT, BLOCK), shape(Y * Z, 4 * PAIR, BLOCK), w_pair, w_shape)
    scratch = [
        pltpu.VMEM((LOCAL, COUNT, BLOCK), BF16),
        pltpu.VMEM((LOCAL, BLOCK, BLOCK), BF16),
        pltpu.VMEM((LOCAL, NBR, BLOCK, BLOCK), BF16),
        pltpu.SemaphoreType.DMA((3,)),
    ]
    q_own, msg, w_own, w_send = call(start_kernel, out, "shhh", scratch, room=60)(
        core, probes, inverses, factor
    )
    ring = [(2 * i, 2 * ((i + 1) % Y)) for i in range(Y)]
    ring += [(2 * i + 1, 2 * ((i - 1) % Y) + 1) for i in range(Y)]
    w_near = lax.ppermute(w_own, ("y", "c"), ring)
    w_far = lax.ppermute(w_send, "y", [(i, (i + 2) % Y) for i in range(Y)])
    got = lax.all_to_all(msg, ROWS, 0, 0, tiled=True)
    swap = [(0, 1), (1, 0)]
    ws = [w_own, w_near, late(lax.ppermute(w_near, "c", swap)), w_far, lax.ppermute(w_far, "c", swap)]

    def rows_of(slots):
        return jnp.sum(jnp.where(owner[None, :] == slots[:, None], iota[None, :], 0), axis=1)

    local_iota = jnp.arange(LOCAL, dtype=jnp.int32)
    way = 1 - 2 * lax.axis_index("c")
    held_y = (my + way * jnp.array([0, -1, 1, 2], jnp.int32)) % Y
    held_flip = jnp.array([0, 0, 1, 0], jnp.int32)
    core = lax.axis_index("c")
    flip = core + held_flip[:, None] + local_iota[None, :]
    slots = (LOCAL * (held_y * Z + mz))[:, None] + flip % LOCAL
    slots = slots.reshape(-1)
    rows = rows_of(slots)
    level = rows // width
    hit = rows[:, None, None] == iota[None, :, None]
    cols = jnp.sum(jnp.where(hit, pattern[None], 0), axis=1)
    src = jnp.sum(jnp.where(cols[..., None] == iota, owner, 0), axis=-1)
    src = jnp.where(cols >= 0, src, -1).reshape(-1)
    dev = src // LOCAL
    bad = -(2**20)
    turn = (way * (dev // Z - my)) % Y
    turn = jnp.where(turn == 3, 1, jnp.where(turn == 0, 0, turn + 1))
    place_z = jnp.where(src >= 0, (dev % Z) * HELD + turn * LOCAL + (src - core - (turn == 2)) % LOCAL, bad)

    def rows_at(place, pad, stride=PAIR):
        col = jnp.arange(pad, dtype=jnp.int32)
        at = jnp.where(col[None, :] < PAIR, place[:, None] * stride + col[None, :], bad)
        return at.reshape(-1)

    def hot(at, size):
        return (at[:, None] == jnp.arange(size, dtype=jnp.int32)[None, :]).astype(BF16)

    def first_at(slot, kind):
        return jnp.where(slot >= 0, (slot // LOCAL) * 4 + kind * LOCAL + slot % LOCAL, bad)

    natural = (((my - jnp.arange(Y, dtype=jnp.int32)) % Y)[:, None] * Z + mz) * LOCAL + local_iota[None, :]
    nat_rows = rows_of(natural.reshape(-1))
    nat_cols = jnp.sum(jnp.where(nat_rows[:, None, None] == iota[None, :, None], pattern[None], 0), axis=1)
    nat_src = jnp.sum(jnp.where(nat_cols[..., None] == iota, owner, 0), axis=-1)
    nat_src = jnp.where(nat_cols >= 0, nat_src, -1).reshape(-1)
    pick1 = jnp.concatenate(
        [
            rows_at(first_at(src, 0), PAD),
            rows_at(first_at(slots, 0), PAD),
        ]
    )
    pick1 = hot(pick1, Y * Z * 4 * PAIR)
    pick_p = hot(rows_at(first_at(nat_src, 1), PAIR), Y * Z * 4 * PAIR)
    got_first = got

    def neighbours(d, since):
        rows = LOCAL * NBR * PAIR
        near = call(neighbour_kernel, shape(rows, BLOCK), "vvh")(
            got_first, pick_p[d * rows : (d + 1) * rows], since
        )
        return lax.ppermute(near, "y", [(i, (i - d) % Y) for i in range(Y)]) if d else near

    at_z = rows_at(place_z, PAD)
    pick_z = hot(at_z, Z * HELD * PAIR)
    put_z = (jnp.arange(Z * HELD * PAIR, dtype=jnp.int32)[:, None] == at_z[None, :]).astype(BF16)
    level_of_src = jnp.where(cols >= 0, cols // width, LEVELS).reshape(-1)
    group = LOCAL * PAIR

    def last_at(slot, good):
        return jnp.where(good, (slot // LOCAL) * (2 * LOCAL) + slot % LOCAL, bad)

    put_last = rows_at(last_at(src, level_of_src == 0), PAD).reshape(1, -1)
    own_last = rows_at(last_at(slots, level > 0), PAIR).reshape(1, -1)

    near_scratch = pltpu.VMEM((WIDE, BLOCK), F32)
    held_scratch = [
        pltpu.VMEM((HELD, NBR, BLOCK, BLOCK), BF16),
        pltpu.SemaphoreType.DMA((HELD,)),
    ]
    pad_scratch = pltpu.VMEM((PAD, BLOCK), F32)
    msg_z = shape(Z, HELD * PAIR, BLOCK)
    held = shape(HELD * PAIR, BLOCK, dtype=F32)
    sums = shape(WIDE, BLOCK, dtype=F32)
    out = (msg_z, held, shape(HELD * PAD, BLOCK, dtype=F32))
    msg, solved, q = call(
        level1_kernel, out, "svv" + "h" * 5, [near_scratch] + held_scratch
    )(level, got, pick1, *ws)
    got = lax.all_to_all(msg, "z", 0, 0, tiled=True)
    near1 = neighbours(1, solved)
    msg, solved = call(
        level2_kernel, (msg_z, held), "svv" + "h" * 5 + "vvhhhh", [near_scratch] + held_scratch
    )(level, got, pick_z, *ws, q, solved, put_z, put_last, own_last, near1)
    got = lax.all_to_all(msg, "z", 0, 0, tiled=True)
    msg, solved, before = call(
        level3_kernel,
        (msg_z, held, sums),
        "svv" + "h" * 5 + "vvv",
        [near_scratch, pad_scratch] + held_scratch,
    )(level, got, pick_z, *ws, q, solved, put_z)
    got = lax.all_to_all(msg, "z", 0, 0, tiled=True)
    msg, t, before = call(
        back2_kernel,
        (msg_z, held, sums),
        "sv" + "h" * 5 + "vvv",
        [near_scratch, pad_scratch] + held_scratch,
    )(level, got, *ws, solved, before, put_z)
    got = lax.all_to_all(msg, "z", 0, 0, tiled=True)
    msg, t = call(
        back1_kernel,
        (shape(Y * Z, 2 * group, BLOCK // 2), held),
        "sv" + "h" * 5 + "vvvv",
        [near_scratch, pad_scratch] + held_scratch,
    )(level, got, *ws, t, before, put_last, own_last)
    got = lax.all_to_all(msg, ROWS, 0, 0, tiled=True)
    mine = (my * Z + mz) * LOCAL + local_iota
    first = (rows_of(mine) < width).astype(jnp.int32)
    out = (shape(LOCAL, COUNT, BLOCK), shape(LOCAL, NBR + 1, BLOCK, BLOCK))
    column = jnp.arange(COUNT, dtype=jnp.int32)
    turn = (((column + PAIR * my) % COUNT)[:, None] == column[None, :]).astype(BF16)
    return call(final_kernel, out, "svvvvvvvvv")(
        first, got, q_own, probes, inverses, turn, neighbours(0, t), near1, neighbours(2, t), neighbours(3, t)
    )


def solution(mesh):
    fine = Mesh(mesh.devices.reshape(Y, Z, -1, 2), ("y", "z", "x", "c"))
    parts = ("x", "c")
    return jax.shard_map(
        body,
        mesh=fine,
        in_specs=(
            P(ROWS, parts, None),
            P(ROWS, None, None, None),
            P(ROWS, None, None),
            P(),
            P(),
        ),
        out_specs=(P(ROWS, parts, None), P(ROWS, parts, None, None)),
        check_vma=False,
    )
```

```python
import functools

import jax
import jax.numpy as jnp
from jax import lax
from jax.experimental import pallas as pl
from jax.experimental.pallas import tpu as pltpu
from jax.sharding import Mesh, PartitionSpec as P

LEVELS = 4
Y, Z = 4, 16
LOCAL, COUNT, BLOCK, NBR = 2, 8, 256, 4
PAIR = COUNT // Y
HELD = Y * LOCAL
PAD = 8
WIDE = HELD * NBR * PAD
ROWS = ("y", "z")
F32, BF16 = jnp.float32, jnp.bfloat16
NT = (((1,), (1,)), ((), ()))
TN = (((0,), (0,)), ((), ()))
VMEM = pl.BlockSpec(memory_space=pltpu.VMEM)
SMEM = pl.BlockSpec(memory_space=pltpu.SMEM)


def call(kernel, out_shape, places, scratch=(), room=52):
    kinds = {"s": SMEM, "v": VMEM, "h": pl.BlockSpec(memory_space=pl.ANY)}
    return pl.pallas_call(
        kernel,
        out_shape=out_shape,
        in_specs=[kinds[p] for p in places],
        out_specs=jax.tree.map(lambda _: VMEM, out_shape),
        scratch_shapes=list(scratch),
        compiler_params=pltpu.CompilerParams(vmem_limit_bytes=room * 2**20),
    )


def shape(*dims, dtype=BF16):
    return jax.ShapeDtypeStruct(dims, dtype)


def dot(a, b, dims=None):
    if dims is None:
        return jnp.dot(a, b, preferred_element_type=F32)
    return lax.dot_general(a, b, dims, preferred_element_type=F32)


def late(value):
    whole = pl.BlockSpec(memory_space=pltpu.HBM)
    return pl.pallas_call(
        lambda value_ref, same_ref: None,
        out_shape=shape(*value.shape),
        in_specs=[whole],
        out_specs=whole,
        input_output_aliases={0: 0},
        compiler_params=pltpu.CompilerParams(vmem_limit_bytes=52 * 2**20),
        cost_estimate=pl.CostEstimate(flops=20000000000, bytes_accessed=2**20, transcendentals=0),
    )(value)


def start_kernel(core_ref, probes_ref, inv_ref, factor_ref, q_ref, msg_ref, w_ref, send_ref, p_ref, d_ref, l_ref, sems):
    load_p = pltpu.make_async_copy(probes_ref, p_ref, sems.at[2])
    load_d = pltpu.make_async_copy(inv_ref, d_ref, sems.at[0])
    load_l = pltpu.make_async_copy(factor_ref, l_ref, sems.at[1])
    load_p.start()
    load_d.start()
    load_l.start()
    load_p.wait()
    load_d.wait()
    parts = []
    for s in range(LOCAL):
        q = dot(p_ref[s], d_ref[s], NT).astype(BF16)
        q_ref[s] = q
        parts.append(q.astype(F32))
    for s in range(LOCAL):
        parts.append(p_ref[s].astype(F32))
    for y in range(Y):
        msg = jnp.concatenate([p[y * PAIR : (y + 1) * PAIR] for p in parts], axis=0).astype(BF16)
        for z in range(Z):
            msg_ref[y * Z + z] = msg
    load_l.wait()
    for i in range(LOCAL):
        slot = (core_ref[0] + i) % LOCAL
        for k in range(NBR):
            w = dot(d_ref[slot], l_ref[slot, k]).astype(BF16)
            w_ref[i, k] = w
            if i == 0:
                send_ref[k] = w


def load_rows(level_ref, lev, w_refs, held_ref, sems):
    waits = []
    for r in range(HELD):
        d, slot = r // LOCAL, r % LOCAL
        source = w_refs[d].at[slot] if d < Y - 1 else w_refs[d + slot]
        copy = pltpu.make_async_copy(source, held_ref.at[r], sems.at[r])

        @pl.when(level_ref[r] == lev)
        def _():
            copy.start()

        waits.append(copy.wait)
    return waits


def forward_rows(level_ref, lev, waits, near_ref, q_ref, w_ref, solved_ref):
    for r in range(HELD):

        @pl.when(level_ref[r] == lev)
        def _():
            waits[r]()
            moved = jnp.zeros((PAD, BLOCK), F32)
            for k in range(NBR):
                at = (r * NBR + k) * PAD
                moved += dot(near_ref[at : at + PAD].astype(BF16), w_ref[r, k], NT)
            value = (q_ref[r * PAD : (r + 1) * PAD] - moved).astype(BF16).astype(F32)
            solved_ref[r * PAIR : (r + 1) * PAIR] = value[:PAIR]


def backward_rows(level_ref, lev, waits, t_ref, pad_ref, w_ref, terms_ref):
    terms_ref[...] = jnp.zeros_like(terms_ref)
    for r in range(HELD):

        @pl.when(level_ref[r] == lev)
        def _():
            if waits is not None:
                waits[r]()
            pad_ref[...] = jnp.zeros_like(pad_ref)
            pad_ref[:PAIR] = t_ref[r * PAIR : (r + 1) * PAIR]
            t = pad_ref[...].astype(BF16)
            for k in range(NBR):
                at = (r * NBR + k) * PAD
                terms_ref[at : at + PAD] = dot(t, w_ref[r, k])


def scatter(place, terms):
    high = terms.astype(BF16)
    return dot(place, high)


def broadcast_to_z(value, msg_ref):
    for z in range(Z):
        msg_ref[z] = value


def neighbour_kernel(got_ref, pick_ref, _, near_ref):
    got = got_ref[...].reshape(Y * Z * 4 * PAIR, BLOCK)
    near_ref[...] = dot(pick_ref[...], got).astype(BF16)


def level1_kernel(level_ref, got_ref, pick_ref, w0_ref, w1_ref, w2_ref, w3_ref, w4_ref, msg_ref, solved_ref, q_ref, near_ref, held_ref, sems):
    waits = load_rows(level_ref, 1, (w0_ref, w1_ref, w2_ref, w3_ref, w4_ref), held_ref, sems)
    got = got_ref[...].reshape(Y * Z * 4 * PAIR, BLOCK)
    near_ref[...] = dot(pick_ref[:WIDE], got)
    q_ref[...] = dot(pick_ref[WIDE : WIDE + HELD * PAD], got)
    for r in range(HELD):
        solved_ref[r * PAIR : (r + 1) * PAIR] = q_ref[r * PAD : r * PAD + PAIR]
    forward_rows(level_ref, 1, waits, near_ref, q_ref, held_ref, solved_ref)
    broadcast_to_z(solved_ref[...].astype(BF16), msg_ref)


def level2_kernel(level_ref, got_ref, pick_ref, w0_ref, w1_ref, w2_ref, w3_ref, w4_ref, q_ref, old_ref, _a, _b, _c, _d, msg_ref, solved_ref, near_ref, held_ref, sems):
    waits = load_rows(level_ref, 2, (w0_ref, w1_ref, w2_ref, w3_ref, w4_ref), held_ref, sems)
    near_ref[...] = dot(pick_ref[...], got_ref[...].reshape(Z * HELD * PAIR, BLOCK))
    solved_ref[...] = old_ref[...]
    forward_rows(level_ref, 2, waits, near_ref, q_ref, held_ref, solved_ref)
    broadcast_to_z(solved_ref[...].astype(BF16), msg_ref)


def level3_kernel(
    level_ref, got_ref, pick_ref, w0_ref, w1_ref, w2_ref, w3_ref, w4_ref, q_ref, old_ref, put_ref,
    msg_ref, solved_ref, terms_ref, near_ref, pad_ref, held_ref, sems):
    waits = load_rows(level_ref, 3, (w0_ref, w1_ref, w2_ref, w3_ref, w4_ref), held_ref, sems)
    near_ref[...] = dot(pick_ref[...], got_ref[...].reshape(Z * HELD * PAIR, BLOCK))
    solved_ref[...] = old_ref[...]
    forward_rows(level_ref, 3, waits, near_ref, q_ref, held_ref, solved_ref)
    backward_rows(level_ref, 3, None, solved_ref, pad_ref, held_ref, terms_ref)
    out = scatter(put_ref[...], terms_ref[...])
    msg_ref[...] = out.astype(BF16).reshape(msg_ref.shape)


def finish_rows(level_ref, lev, got_ref, old_ref, t_ref):
    acc = jnp.sum(got_ref[...].astype(F32), axis=0)
    t_ref[...] = old_ref[...]
    for r in range(HELD):

        @pl.when(level_ref[r] == lev)
        def _():
            rows = slice(r * PAIR, (r + 1) * PAIR)
            t_ref[rows] = (old_ref[rows] - acc[rows]).astype(BF16).astype(F32)


def back2_kernel(
    level_ref, got_ref, w0_ref, w1_ref, w2_ref, w3_ref, w4_ref, old_ref, before_ref, put_ref,
    msg_ref, t_ref, sums_ref, terms_ref, pad_ref, held_ref, sems):
    waits = load_rows(level_ref, 2, (w0_ref, w1_ref, w2_ref, w3_ref, w4_ref), held_ref, sems)
    finish_rows(level_ref, 2, got_ref, old_ref, t_ref)
    backward_rows(level_ref, 2, waits, t_ref, pad_ref, held_ref, terms_ref)
    sums_ref[...] = before_ref[...] + terms_ref[...]
    out = scatter(put_ref[...], sums_ref[...])
    msg_ref[...] = out.astype(BF16).reshape(msg_ref.shape)


def back1_kernel(
    level_ref, got_ref, w0_ref, w1_ref, w2_ref, w3_ref, w4_ref, old_ref, before_ref, put_ref, own_ref, msg_ref, t_ref, terms_ref, pad_ref, held_ref, sems):
    waits = load_rows(level_ref, 1, (w0_ref, w1_ref, w2_ref, w3_ref, w4_ref), held_ref, sems)
    finish_rows(level_ref, 1, got_ref, old_ref, t_ref)
    backward_rows(level_ref, 1, waits, t_ref, pad_ref, held_ref, terms_ref)
    sums = before_ref[...] + terms_ref[...]
    t = t_ref[...].astype(BF16)
    half = BLOCK // 2
    group = LOCAL * PAIR
    size = Y * Z * 2 * group

    def hot(at, h):
        rows = lax.broadcasted_iota(jnp.int32, (size, at.shape[1]), 0)
        return jnp.where(rows == at + h * group, 1.0, 0.0).astype(BF16)

    put_at, own_at = put_ref[...], own_ref[...]
    left = scatter(hot(put_at, 0), sums[:, :half]) + dot(hot(own_at, 0), t[:, :half])
    right = scatter(hot(put_at, 1), sums[:, half:]) + dot(hot(own_at, 1), t[:, half:])
    msg_ref[...] = (left + right).astype(BF16).reshape(msg_ref.shape)


def final_kernel(first_ref, got_ref, q_ref, probes_ref, inv_ref, turn_ref, near0_ref, near1_ref, near2_ref, near3_ref, x_ref, sel_ref):
    near_refs = (near0_ref, near1_ref, near2_ref, near3_ref)
    group = LOCAL * PAIR
    sums = []
    for y in range(Y):
        v = jnp.sum(got_ref[y * Z : (y + 1) * Z].astype(F32), axis=0)
        sums.append(jnp.concatenate([v[:group], v[group:]], axis=1))
    for s in range(LOCAL):
        acc = jnp.concatenate([v[s * PAIR : (s + 1) * PAIR] for v in sums], axis=0)
        base = jnp.where(first_ref[s] == 1, q_ref[s].astype(F32) - acc, acc)
        x = dot(base.astype(BF16), inv_ref[s]).astype(BF16)
        x_ref[s] = x
        turned = dot(turn_ref[...], x).astype(BF16)
        for k in range(NBR):
            at = (s * NBR + k) * PAIR
            near = jnp.concatenate(
                [ref[at : at + PAIR].astype(F32) for ref in near_refs], axis=0
            ).astype(BF16)
            sel_ref[s, k] = (dot(turned, near, TN) * (1.0 / COUNT)).astype(BF16)
        sel_ref[s, NBR] = (dot(x, probes_ref[s], TN) * (1.0 / COUNT)).astype(BF16)


def body(probes, factor, inverses, pattern, owner):
    my, mz = lax.axis_index("y"), lax.axis_index("z")
    total = owner.shape[0]
    width = total // LEVELS
    iota = jnp.arange(total, dtype=jnp.int32)

    core = lax.axis_index("c").reshape(1)
    w_shape = shape(NBR, BLOCK, BLOCK)
    w_pair = shape(LOCAL, NBR, BLOCK, BLOCK)
    out = (shape(LOCAL, COUNT, BLOCK), shape(Y * Z, 4 * PAIR, BLOCK), w_pair, w_shape)
    scratch = [
        pltpu.VMEM((LOCAL, COUNT, BLOCK), BF16),
        pltpu.VMEM((LOCAL, BLOCK, BLOCK), BF16),
        pltpu.VMEM((LOCAL, NBR, BLOCK, BLOCK), BF16),
        pltpu.SemaphoreType.DMA((3,)),
    ]
    q_own, msg, w_own, w_send = call(start_kernel, out, "shhh", scratch, room=60)(
        core, probes, inverses, factor
    )
    ring = [(2 * i, 2 * ((i + 1) % Y)) for i in range(Y)]
    ring += [(2 * i + 1, 2 * ((i - 1) % Y) + 1) for i in range(Y)]
    w_near = lax.ppermute(w_own, ("y", "c"), ring)
    w_far = lax.ppermute(w_send, "y", [(i, (i + 2) % Y) for i in range(Y)])
    got = lax.all_to_all(msg, ROWS, 0, 0, tiled=True)
    swap = [(0, 1), (1, 0)]
    ws = [w_own, w_near, late(lax.ppermute(w_near, "c", swap)), w_far, lax.ppermute(w_far, "c", swap)]

    def rows_of(slots):
        return jnp.sum(jnp.where(owner[None, :] == slots[:, None], iota[None, :], 0), axis=1)

    local_iota = jnp.arange(LOCAL, dtype=jnp.int32)
    way = 1 - 2 * lax.axis_index("c")
    held_y = (my + way * jnp.array([0, -1, 1, 2], jnp.int32)) % Y
    held_flip = jnp.array([0, 0, 1, 0], jnp.int32)
    core = lax.axis_index("c")
    flip = core + held_flip[:, None] + local_iota[None, :]
    slots = (LOCAL * (held_y * Z + mz))[:, None] + flip % LOCAL
    slots = slots.reshape(-1)
    rows = rows_of(slots)
    level = rows // width
    hit = rows[:, None, None] == iota[None, :, None]
    cols = jnp.sum(jnp.where(hit, pattern[None], 0), axis=1)
    src = jnp.sum(jnp.where(cols[..., None] == iota, owner, 0), axis=-1)
    src = jnp.where(cols >= 0, src, -1).reshape(-1)
    dev = src // LOCAL
    bad = -(2**20)
    turn = (way * (dev // Z - my)) % Y
    turn = jnp.where(turn == 3, 1, jnp.where(turn == 0, 0, turn + 1))
    place_z = jnp.where(src >= 0, (dev % Z) * HELD + turn * LOCAL + (src - core - (turn == 2)) % LOCAL, bad)

    def rows_at(place, pad, stride=PAIR):
        col = jnp.arange(pad, dtype=jnp.int32)
        at = jnp.where(col[None, :] < PAIR, place[:, None] * stride + col[None, :], bad)
        return at.reshape(-1)

    def hot(at, size):
        return (at[:, None] == jnp.arange(size, dtype=jnp.int32)[None, :]).astype(BF16)

    def first_at(slot, kind):
        return jnp.where(slot >= 0, (slot // LOCAL) * 4 + kind * LOCAL + slot % LOCAL, bad)

    natural = (((my - jnp.arange(Y, dtype=jnp.int32)) % Y)[:, None] * Z + mz) * LOCAL + local_iota[None, :]
    nat_rows = rows_of(natural.reshape(-1))
    nat_cols = jnp.sum(jnp.where(nat_rows[:, None, None] == iota[None, :, None], pattern[None], 0), axis=1)
    nat_src = jnp.sum(jnp.where(nat_cols[..., None] == iota, owner, 0), axis=-1)
    nat_src = jnp.where(nat_cols >= 0, nat_src, -1).reshape(-1)
    pick1 = jnp.concatenate(
        [
            rows_at(first_at(src, 0), PAD),
            rows_at(first_at(slots, 0), PAD),
        ]
    )
    pick1 = hot(pick1, Y * Z * 4 * PAIR)
    pick_p = hot(rows_at(first_at(nat_src, 1), PAIR), Y * Z * 4 * PAIR)
    got_first = got

    def neighbours(d, since):
        rows = LOCAL * NBR * PAIR
        near = call(neighbour_kernel, shape(rows, BLOCK), "vvh")(
            got_first, pick_p[d * rows : (d + 1) * rows], since
        )
        return lax.ppermute(near, "y", [(i, (i - d) % Y) for i in range(Y)]) if d else near

    at_z = rows_at(place_z, PAD)
    pick_z = hot(at_z, Z * HELD * PAIR)
    put_z = (jnp.arange(Z * HELD * PAIR, dtype=jnp.int32)[:, None] == at_z[None, :]).astype(BF16)
    level_of_src = jnp.where(cols >= 0, cols // width, LEVELS).reshape(-1)
    group = LOCAL * PAIR

    def last_at(slot, good):
        return jnp.where(good, (slot // LOCAL) * (2 * LOCAL) + slot % LOCAL, bad)

    put_last = rows_at(last_at(src, level_of_src == 0), PAD).reshape(1, -1)
    own_last = rows_at(last_at(slots, level > 0), PAIR).reshape(1, -1)

    near_scratch = pltpu.VMEM((WIDE, BLOCK), F32)
    held_scratch = [
        pltpu.VMEM((HELD, NBR, BLOCK, BLOCK), BF16),
        pltpu.SemaphoreType.DMA((HELD,)),
    ]
    pad_scratch = pltpu.VMEM((PAD, BLOCK), F32)
    msg_z = shape(Z, HELD * PAIR, BLOCK)
    held = shape(HELD * PAIR, BLOCK, dtype=F32)
    sums = shape(WIDE, BLOCK, dtype=F32)
    out = (msg_z, held, shape(HELD * PAD, BLOCK, dtype=F32))
    msg, solved, q = call(
        level1_kernel, out, "svv" + "h" * 5, [near_scratch] + held_scratch
    )(level, got, pick1, *ws)
    got = lax.all_to_all(msg, "z", 0, 0, tiled=True)
    near1 = neighbours(1, solved)
    msg, solved = call(
        level2_kernel, (msg_z, held), "svv" + "h" * 5 + "vvhhhh", [near_scratch] + held_scratch
    )(level, got, pick_z, *ws, q, solved, put_z, put_last, own_last, near1)
    got = lax.all_to_all(msg, "z", 0, 0, tiled=True)
    msg, solved, before = call(
        level3_kernel,
        (msg_z, held, sums),
        "svv" + "h" * 5 + "vvv",
        [near_scratch, pad_scratch] + held_scratch,
    )(level, got, pick_z, *ws, q, solved, put_z)
    got = lax.all_to_all(msg, "z", 0, 0, tiled=True)
    msg, t, before = call(
        back2_kernel,
        (msg_z, held, sums),
        "sv" + "h" * 5 + "vvv",
        [near_scratch, pad_scratch] + held_scratch,
    )(level, got, *ws, solved, before, put_z)
    got = lax.all_to_all(msg, "z", 0, 0, tiled=True)
    msg, t = call(
        back1_kernel,
        (shape(Y * Z, 2 * group, BLOCK // 2), held),
        "sv" + "h" * 5 + "vvvv",
        [near_scratch, pad_scratch] + held_scratch,
    )(level, got, *ws, t, before, put_last, own_last)
    got = lax.all_to_all(msg, ROWS, 0, 0, tiled=True)
    mine = (my * Z + mz) * LOCAL + local_iota
    first = (rows_of(mine) < width).astype(jnp.int32)
    out = (shape(LOCAL, COUNT, BLOCK), shape(LOCAL, NBR + 1, BLOCK, BLOCK))
    column = jnp.arange(COUNT, dtype=jnp.int32)
    turn = (((column + PAIR * my) % COUNT)[:, None] == column[None, :]).astype(BF16)
    return call(final_kernel, out, "svvvvvvvvv")(
        first, got, q_own, probes, inverses, turn, neighbours(0, t), near1, neighbours(2, t), neighbours(3, t)
    )


def solution(mesh):
    fine = Mesh(mesh.devices.reshape(Y, Z, -1, 2), ("y", "z", "x", "c"))
    parts = ("x", "c")
    return jax.shard_map(
        body,
        mesh=fine,
        in_specs=(
            P(ROWS, parts, None),
            P(ROWS, None, None, None),
            P(ROWS, None, None),
            P(),
            P(),
        ),
        out_specs=(P(ROWS, parts, None), P(ROWS, parts, None, None)),
        check_vma=False,
    )
```
